256 devices in a mesh: dom: 32 (over z, y), rep: 8 (over x, core).
Axes of the slice: x: 4, y: 4, z: 8, core: 2. Of those that a mesh axis runs over, the one named last changes fastest.
Arguments:
- features: bfloat16 [8, 128, 64, 256], P('rep', 'dom'), may hold values from -6 to 6
- coords: int32 [8, 3, 8192], P('rep', None, 'dom'), may hold values from 0 to 47
- kernel_points: float32 [15, 3], replicated, may hold values from -1.2 to 1.2
- weights: bfloat16 [3840, 256], replicated, may hold values from -0.09375 to 0.09375
- support_slot: int32 [8, 128, 4], P('rep', 'dom'), may hold values from 0 to 13, as said below
- slot_mask: int32 [8, 128, 4, 64, 64], P('rep', 'dom'), may hold values 0 or 1
- send_leaf: int32 [8, 32, 5, 2], P('rep', 'dom'), may hold values from 0 to 3
- cotangent: bfloat16 [8, 128, 64, 256], P('rep', 'dom'), may hold values from -6 to 6
Outputs:
- output: bfloat16 [8, 128, 64, 256], P('rep', 'dom')
- grad_features: bfloat16 [8, 128, 64, 256], P('rep', 'dom')
- grad_weight: float32 [3840, 256], replicated
The draws below stay inside these ranges and needn't reach their ends.
Inputs may be any that keep to these rules, and one draw needn't show every extreme that they name: `support_slot`: entries below 4 name the device's own leaves; entry 4 + b * 2 + t names the t-th leaf offered by the partner at bit b, and every such entry is named by some slot of the device; slot 0 of each query leaf names the leaf itself.
All inputs are finite; a program needn't handle non-finite values. No bound on the sum of `slot_mask` on one device may be relied on, other than what follows from the above.
Results may differ from the reference program's by a relative error of at most 0.0057.
Values may be sent and summed in bfloat16 or wider, within the bound.
A program may use at most 64 MiB of HBM per device.

```python
import jax
import jax.numpy as jnp
from jax import lax

C = 256
CO = 256
K = 15
PTS = 64
NEAR = 4
BOUND = 2
LEAF_DEV = 4
ROUNDS = 5
LEAVES = 128
POINTS = 8192
N_DOM = 32
N_REP = 8


def draw_support_slot(key, part):
    key = jax.random.fold_in(key, 7)
    device_keys = jax.random.split(key, N_REP * N_DOM)

    def one_device(device_key):
        first_key, second_key = jax.random.split(device_key)
        table = jax.random.randint(first_key, (LEAF_DEV, NEAR), 0, LEAF_DEV, dtype=jnp.int32)
        table = table.at[:, 0].set(jnp.arange(LEAF_DEV, dtype=jnp.int32))
        shuffled = jax.random.permutation(second_key, LEAF_DEV).astype(jnp.int32)
        received = jnp.arange(ROUNDS * BOUND, dtype=jnp.int32)
        table = table.at[shuffled[received % LEAF_DEV], 1 + received // LEAF_DEV].set(LEAF_DEV + received)
        return table
    return jax.vmap(one_device)(device_keys).reshape(N_REP, N_DOM * LEAF_DEV, NEAR)


def touch_ends(values, own_key, low, top_value):
    longest = values.shape.index(max(values.shape))
    spots = []
    for shift in (0, 1):
        where = [jax.random.randint(jax.random.fold_in(own_key, axis), (), 0, length) for axis, length in enumerate(values.shape)]
        where[longest] = (where[longest] + shift) % values.shape[longest]
        spots.append(tuple(where))
    return values.at[spots[0]].set(low).at[spots[1]].set(top_value)


def shard_levels(stream_key, shape, shards, smallest, largest):
    loudness, own = 1.0, jax.random.fold_in(stream_key, 6)
    for position, shards_of in shards:
        draws = jnp.exp(jax.random.uniform(jax.random.fold_in(own, position), (shards_of,), jnp.float32, smallest / len(shards), largest / len(shards)))
        loudness = loudness * jnp.repeat(draws, shape[position] // shards_of).reshape([-1 if axis == position else 1 for axis in range(len(shape))])
    return loudness


def noise(key, dims, width, limit, cuts=(), kind=jnp.bfloat16):
    entries = jax.random.normal(key, dims, jnp.float32) * width
    if len(cuts) > 0:
        entries = shard_levels(key, dims, cuts, -0.22, 0.18) * entries
    return jnp.clip(entries, min=-limit, max=limit).astype(kind)


def setup_inputs(seed: int = 0) -> dict:
    keys = jax.random.split(jax.random.key(seed), 9)
    return {
        "features": noise(keys[0], (N_REP, LEAVES, PTS, C), 1.0, 6.0, ((0, 8), (1, 32))),
        "coords": touch_ends(jax.random.randint(keys[1], (N_REP, 3, POINTS), 0, 48), jax.random.fold_in(keys[1], 1), 0, 47).astype(jnp.int32),
        "kernel_points": jnp.clip(jax.random.uniform(keys[2], (K, 3), jnp.float32, -1.2, 1.2), -1.2, 1.2),
        "weights": noise(keys[3], (K * C, CO), (K * C) ** -0.5, 0.09375),
        "support_slot": draw_support_slot(jax.random.fold_in(keys[8], 71), 0),
        "slot_mask": touch_ends((jax.random.randint(keys[5], (N_REP, LEAVES, NEAR, PTS, PTS), 0, 2) < 1).astype(jnp.int32), jax.random.fold_in(keys[5], 1), 0, 1),
        "send_leaf": touch_ends(jax.random.randint(keys[6], (N_REP, N_DOM, ROUNDS, BOUND), 0, LEAF_DEV), jax.random.fold_in(keys[6], 1), 0, LEAF_DEV - 1).astype(jnp.int32),
        "cotangent": noise(keys[7], (N_REP, LEAVES, PTS, CO), 1.0, 6.0, ((0, 8), (1, 32))),
    }


QUANT = 0.0625
EPSILON = 1e-06

def correlation(query_pos, support_pos, slot_masks, kernel_points):
    squared = jnp.zeros((query_pos.shape[1], kernel_points.shape[0], query_pos.shape[2], support_pos.shape[2]), jnp.float32)
    for component in range(3):
        difference = support_pos[component][:, None, None, :] - query_pos[component][:, None, :, None] - kernel_points[:, component][None, :, None, None]
        squared = squared + difference * difference
    distance = jnp.sqrt(squared + EPSILON)
    weight_map = jnp.maximum(1.0 - distance, 0.0) * slot_masks.astype(jnp.float32)[:, None, :, :]
    return weight_map.astype(jnp.bfloat16)

def reference(features, coords, kernel_points, weights, support_slot, slot_mask, send_leaf, cotangent):
    kernels = kernel_points.shape[0]
    channels = features.shape[-1]
    weight_cube = weights.astype(jnp.float32).reshape(kernels, channels, -1)
    leaf_total = N_DOM * LEAF_DEV
    device_ids = jnp.arange(N_DOM, dtype=jnp.int32)

    def one_scan(scan_inputs):
        scan_feats, scan_coords, scan_slots, scan_masks, scan_sends, scan_upstream = scan_inputs
        positions = (scan_coords.astype(jnp.float32) * QUANT).reshape(3, leaf_total, PTS)
        pool_parts = [device_ids[:, None] * LEAF_DEV + jnp.arange(LEAF_DEV, dtype=jnp.int32)[None, :]]
        for bit_index in range(ROUNDS):
            partner = jnp.bitwise_xor(device_ids, 1 << bit_index).astype(jnp.int32)
            pool_parts.append(partner[:, None] * LEAF_DEV + scan_sends[partner, bit_index])
        pool_index = jnp.concatenate(pool_parts, 1).astype(jnp.int32)
        slot_table = scan_slots.reshape(N_DOM, LEAF_DEV, NEAR)
        global_slots = jax.vmap(lambda pool_row, table_row: pool_row[table_row])(pool_index, slot_table)

        def one_device(device_inputs):
            query_pos, support_index, device_masks, device_upstream = device_inputs
            support_feats = scan_feats[support_index].astype(jnp.float32)
            pieces = []
            for slot_index in range(NEAR):
                pieces.append(correlation(query_pos, positions[:, support_index[:, slot_index]], device_masks[:, slot_index], kernel_points))
            correlated = lax.optimization_barrier(jnp.stack(pieces, 1))
            corr_wide = correlated.astype(jnp.float32)
            summed = jnp.einsum('lnkij,lnjc->lkic', corr_wide, support_feats)
            summed_low = lax.optimization_barrier(summed.astype(jnp.bfloat16))
            summed_wide = summed_low.astype(jnp.float32)
            output = jnp.einsum('lkic,kco->lio', summed_wide, weight_cube).astype(jnp.bfloat16)
            upstream_wide = device_upstream.astype(jnp.float32)
            grad_low = lax.optimization_barrier(jnp.einsum('lio,kco->lkic', upstream_wide, weight_cube).astype(jnp.bfloat16))
            grad_summed = grad_low.astype(jnp.float32)
            grad_local = jnp.einsum('lkic,lio->kco', summed_wide, upstream_wide)
            grad_support = jnp.einsum('lnkij,lkic->lnjc', corr_wide, grad_summed)
            return (output, grad_local, grad_support)
        query_positions = positions.reshape(3, N_DOM, LEAF_DEV, PTS).transpose(1, 0, 2, 3)
        outputs, grad_locals, grad_supports = lax.map(one_device, (query_positions, global_slots, scan_masks.reshape(N_DOM, LEAF_DEV, NEAR, PTS, PTS), scan_upstream.reshape(N_DOM, LEAF_DEV, PTS, -1)))
        grad_leaves = jax.ops.segment_sum(grad_supports.reshape(-1, PTS, channels), global_slots.reshape(-1), num_segments=leaf_total)
        return (outputs.reshape(leaf_total, PTS, -1), grad_leaves.astype(jnp.bfloat16), lax.optimization_barrier(jnp.sum(grad_locals, 0)))
    outputs, grad_feats, grad_parts = lax.map(one_scan, (features, coords, support_slot, slot_mask, send_leaf, cotangent))
    grad_weight = (lax.optimization_barrier(jnp.sum(grad_parts, 0)) / (N_REP * N_DOM)).reshape(kernels * channels, -1)
    return (outputs, grad_feats, grad_weight)
```

```python
import functools

import jax
import jax.numpy as jnp
from jax import lax
from jax.experimental import pallas as pl
from jax.experimental.pallas import tpu as pltpu
from jax.sharding import PartitionSpec as P

QUANT = 0.0625
EPSILON = 1e-06
CORES = 2
NY = 4
MESH = pl.DeviceIdType.MESH


def swapped(block, axis, stride):
    count = lax.axis_size(axis)
    route = []
    for low in range(count):
        high = low | 1 << stride
        if high != low and high < count:
            route += [(low, high), (high, low)]
    return lax.ppermute(block, axis, route)


def place():
    dom, rep = lax.axis_index("dom"), lax.axis_index("rep")
    return rep // CORES, lax.rem(dom, NY), dom // NY, lax.rem(rep, CORES)


def device(x, y, z, core):
    return (z * NY + y, x * CORES + core)


def greet(others):
    barrier = pltpu.get_barrier_semaphore()
    for other in others:
        pl.semaphore_signal(barrier, inc=1, device_id=other, device_id_type=MESH)
    pl.semaphore_wait(barrier, len(others))


def remote(src, dst, send, recv, other):
    copy = pltpu.make_async_remote_copy(
        src_ref=src, dst_ref=dst, send_sem=send, recv_sem=recv, device_id=other, device_id_type=MESH
    )
    copy.start()
    return copy


def around(position, count):
    return [lax.rem(position + step, count) for step in range(1, count)]


def sum_kernel(nx, nz, kernels, p, final, mine, got0, got_first, part, got_second, slab, got_z, piece, gather_z, gather_second, send, recv):
    x, y, z, core = place()
    sibling = device(x, y, z, 1 - core)
    lanes = {"x": (x, nx, lambda o: device(o, y, z, core)), "y": (y, NY, lambda o: device(x, o, z, core))}
    z_ring = [(o, device(x, y, o, core)) for o in around(z, nz)]
    others = [sibling] + [d for _, d in z_ring]
    for at, count, to in lanes.values():
        others += [to(o) for o in around(at, count)]
    greet(others)

    rows = p.shape[2]
    per_z = gather_z.shape[0] // nz
    half = (kernels + 1) // 2
    groups = [(0, half, "x", "y"), (half, kernels - half, "y", "x")]
    number = [0]

    def push(src, dst, other):
        index = number[0]
        number[0] += 1
        return remote(src, dst, send.at[index], recv.at[index], other)

    started = []

    def wait_all(copies):
        for copy in copies:
            copy.wait_recv()
        started.extend(copies)

    copies = []
    for k0, nk, _, _ in groups:
        copies.append([push(p.at[1 - core, pl.ds(k0, nk)], got0.at[pl.ds(k0, nk)], sibling)])
    firsts = []
    for (k0, nk, first, _), copy in zip(groups, copies):
        wait_all(copy)

        def add0(k, _):
            total = p[core, k].astype(jnp.float32) + got0[k].astype(jnp.float32)
            mine[k] = total.astype(jnp.bfloat16)
            return 0

        lax.fori_loop(k0, k0 + nk, add0, 0)
        at, count, to = lanes[first]
        block = rows // count
        firsts.append([
            push(
                mine.at[pl.ds(k0, nk), pl.ds(pl.multiple_of(o * block, block), block)],
                got_first.at[step, pl.ds(k0, nk)],
                to(o),
            )
            for step, o in enumerate(around(at, count))
        ])
    seconds = []
    for (k0, nk, first, second), copy in zip(groups, firsts):
        wait_all(copy)
        at, count, _ = lanes[first]
        block = rows // count
        own = pl.ds(pl.multiple_of(at * block, block), block)

        def add1(k, _):
            total = mine[k, own].astype(jnp.float32)
            for step in range(count - 1):
                total = total + got_first[step, k].astype(jnp.float32)
            part[k] = total.astype(jnp.bfloat16)
            return 0

        lax.fori_loop(k0, k0 + nk, add1, 0)
        at, count, to = lanes[second]
        block = part.shape[1] // count
        seconds.append([
            push(
                part.at[pl.ds(k0, nk), pl.ds(pl.multiple_of(o * block, block), block)],
                got_second.at[step, pl.ds(k0, nk)],
                to(o),
            )
            for step, o in enumerate(around(at, count))
        ])
    for k in range(kernels, slab.shape[0]):
        slab[k] = jnp.zeros(slab.shape[1:], slab.dtype)
    for (k0, nk, _, second), copy in zip(groups, seconds):
        wait_all(copy)
        at, count, _ = lanes[second]
        block = part.shape[1] // count
        own = pl.ds(pl.multiple_of(at * block, block), block)

        def add2(k, _):
            total = part[k, own].astype(jnp.float32)
            for step in range(count - 1):
                total = total + got_second[step, k].astype(jnp.float32)
            slab[k] = total.astype(jnp.bfloat16)
            return 0

        lax.fori_loop(k0, k0 + nk, add2, 0)
    wait_all([])
    copies = [
        push(slab.at[pl.ds(o * per_z, per_z)], got_z.at[step], other) for step, (o, other) in enumerate(z_ring)
    ]
    wait_all(copies)
    own_z = pl.ds(z * per_z, per_z)
    total = slab[own_z].astype(jnp.float32)
    for step in range(nz - 1):
        total = total + got_z[step].astype(jnp.float32)
    devices = nx * NY * nz * CORES
    piece[...] = (total / devices).astype(jnp.bfloat16)
    copies = [push(piece, gather_z.at[own_z], other) for _, other in z_ring]
    gather_z[own_z] = piece[...]
    wait_all(copies)
    backs = []
    for k0, nk, _, second in groups:
        at, count, to = lanes[second]
        block = part.shape[1] // count
        own = pl.ds(pl.multiple_of(at * block, block), block)
        backs.append([
            push(gather_z.at[pl.ds(k0, nk)], gather_second.at[pl.ds(k0, nk), own], to(o)) for o in around(at, count)
        ])
        gather_second[pl.ds(k0, nk), own] = gather_z[pl.ds(k0, nk)]
    fronts = []
    for (k0, nk, first, _), copy in zip(groups, backs):
        wait_all(copy)
        at, count, to = lanes[first]
        block = rows // count
        own = pl.ds(pl.multiple_of(at * block, block), block)
        fronts.append([
            push(gather_second.at[pl.ds(k0, nk)], final.at[core, pl.ds(k0, nk), own], to(o)) for o in around(at, count)
        ])
        final[core, pl.ds(k0, nk), own] = gather_second[pl.ds(k0, nk)]
    lasts = []
    for (k0, nk, _, _), copy in zip(groups, fronts):
        wait_all(copy)
        half_ref = final.at[core, pl.ds(k0, nk)]
        lasts.append(push(half_ref, half_ref, sibling))
    wait_all(lasts)
    for copy in started:
        copy.wait_send()


def summed_weights(partial, nx, nz):
    _, kernels, rows, lanes = partial.shape
    per_z = -(-kernels // nz)
    bf16 = jnp.bfloat16
    wide = max(nx, NY)
    copies = 2 * (1 + (nx - 1) + (NY - 1)) * 2 + 2 * (nz - 1)
    narrow = min(nx, NY)
    return pl.pallas_call(
        functools.partial(sum_kernel, nx, nz, kernels),
        out_shape=jax.ShapeDtypeStruct(partial.shape, bf16),
        in_specs=[pl.BlockSpec(memory_space=pltpu.VMEM)],
        out_specs=pl.BlockSpec(memory_space=pltpu.VMEM),
        scratch_shapes=[
            pltpu.VMEM((kernels, rows, lanes), bf16),
            pltpu.VMEM((kernels, rows, lanes), bf16),
            pltpu.VMEM((wide - 1, kernels, rows // narrow, lanes), bf16),
            pltpu.VMEM((kernels, rows // narrow, lanes), bf16),
            pltpu.VMEM((wide - 1, kernels, rows // (nx * NY), lanes), bf16),
            pltpu.VMEM((per_z * nz, rows // (nx * NY), lanes), bf16),
            pltpu.VMEM((nz - 1, per_z, rows // (nx * NY), lanes), bf16),
            pltpu.VMEM((per_z, rows // (nx * NY), lanes), bf16),
            pltpu.VMEM((per_z * nz, rows // (nx * NY), lanes), bf16),
            pltpu.VMEM((kernels, rows // narrow, lanes), bf16),
            pltpu.SemaphoreType.DMA((copies,)),
            pltpu.SemaphoreType.DMA((copies,)),
        ],
        compiler_params=pltpu.CompilerParams(
            collective_id=0, has_side_effects=True, vmem_limit_bytes=32 * 1024 * 1024
        ),
        name="sum_weights",
    )(partial)


def correlation(query_pos, support_pos, slot_masks, kernel_points):
    squared = jnp.zeros(
        (query_pos.shape[1], kernel_points.shape[0], query_pos.shape[2], support_pos.shape[2]),
        jnp.float32,
    )
    for component in range(3):
        difference = (
            support_pos[component][:, None, None, :]
            - query_pos[component][:, None, :, None]
            - kernel_points[:, component][None, :, None, None]
        )
        squared = squared + difference * difference
    distance = jnp.sqrt(squared + EPSILON)
    weight_map = jnp.maximum(1.0 - distance, 0.0) * slot_masks.astype(jnp.float32)[:, None, :, :]
    return weight_map.astype(jnp.bfloat16)


def shards(features, coords, kernel_points, weights, support_slot, slot_mask, send_leaf, cotangent):
    leaf_feats = features[0]
    leaf_count, points, channels = leaf_feats.shape
    kernels = kernel_points.shape[0]
    positions = (coords[0].astype(jnp.float32) * QUANT).reshape(3, leaf_count, points)
    rounds = lax.axis_size("dom").bit_length() - 1
    send_table = send_leaf[0, 0]
    bound_count = send_table.shape[1]
    got_feats = []
    got_pos = []
    for bit_index in range(rounds):
        got_feats.append(swapped(leaf_feats[send_table[bit_index]], "dom", bit_index))
        got_pos.append(swapped(positions[:, send_table[bit_index]].astype(jnp.bfloat16), "dom", bit_index))
    pool_feats = jnp.concatenate([leaf_feats] + got_feats, 0)
    pool_pos = jnp.concatenate([positions] + [piece.astype(jnp.float32) for piece in got_pos], 1)
    slot_table = support_slot[0]
    near_count = slot_table.shape[1]
    support_feats = pool_feats[slot_table]
    pieces = []
    for slot_index in range(near_count):
        pieces.append(
            correlation(
                positions,
                pool_pos[:, slot_table[:, slot_index]],
                slot_mask[0][:, slot_index],
                kernel_points,
            )
        )
    correlated = jnp.stack(pieces, 1)
    summed = jnp.einsum(
        "lnkij,lnjc->lkic", correlated, support_feats, preferred_element_type=jnp.float32
    )
    summed_low = summed.astype(jnp.bfloat16)
    weight_cube = weights.reshape(kernels, channels, -1)
    output = jnp.einsum(
        "lkic,kco->lio", summed_low, weight_cube, preferred_element_type=jnp.float32
    ).astype(jnp.bfloat16)
    upstream = cotangent[0]
    grad_summed = jnp.einsum(
        "lio,kco->lkic", upstream, weight_cube, preferred_element_type=jnp.float32
    ).astype(jnp.bfloat16)
    grad_local = jnp.einsum(
        "lkic,lio->kco", summed_low, upstream, preferred_element_type=jnp.float32
    ).astype(jnp.bfloat16)
    halves = grad_local.reshape(kernels, channels, CORES, -1).transpose(2, 0, 1, 3)
    nx, nz = lax.axis_size("rep") // CORES, lax.axis_size("dom") // NY
    total = summed_weights(halves, nx, nz)
    grad_weight = total.transpose(1, 2, 0, 3).reshape(kernels * channels, -1).astype(jnp.float32)
    grad_support = jnp.einsum(
        "lnkij,lkic->lnjc", correlated, grad_summed, preferred_element_type=jnp.float32
    )
    pool_size = leaf_count + rounds * bound_count
    selector = (
        jnp.arange(pool_size, dtype=jnp.int32)[:, None] == slot_table.reshape(-1)[None, :]
    ).astype(jnp.float32)
    grad_pool = jnp.dot(
        selector,
        grad_support.reshape(leaf_count * near_count, points * channels),
        precision=lax.Precision.HIGHEST,
        preferred_element_type=jnp.float32,
    )
    grad_pool = grad_pool.reshape(pool_size, points, channels)
    grad_leaves = grad_pool[:leaf_count]
    for bit_index in range(rounds):
        offset = leaf_count + bit_index * bound_count
        returned = swapped(grad_pool[offset : offset + bound_count].astype(jnp.bfloat16), "dom", bit_index)
        back_select = (
            jnp.arange(leaf_count, dtype=jnp.int32)[:, None] == send_table[bit_index][None, :]
        ).astype(jnp.bfloat16)
        grad_leaves = grad_leaves + jnp.dot(
            back_select,
            returned.reshape(bound_count, -1),
            preferred_element_type=jnp.float32,
        ).reshape(leaf_count, points, channels)
    return (output[None], grad_leaves.astype(jnp.bfloat16)[None], grad_weight)


def solution(mesh):
    in_specs = (
        P("rep", "dom", None, None),
        P("rep", None, "dom"),
        P(),
        P(),
        P("rep", "dom", None),
        P("rep", "dom", None, None, None),
        P("rep", "dom", None, None),
        P("rep", "dom", None, None),
    )
    out_specs = (P("rep", "dom", None, None), P("rep", "dom", None, None), P())
    return jax.shard_map(shards, mesh=mesh, in_specs=in_specs, out_specs=out_specs, check_vma=False)
```

```python
import functools

import jax
import jax.numpy as jnp
from jax import lax
from jax.experimental import pallas as pl
from jax.experimental.pallas import tpu as pltpu
from jax.sharding import PartitionSpec as P

QUANT = 0.0625
EPSILON = 1e-06
CORES = 2
NY = 4
CHUNK = 8
MESH = pl.DeviceIdType.MESH
F32, BF16 = jnp.float32, jnp.bfloat16


def place():
    dom, rep = lax.axis_index("dom"), lax.axis_index("rep")
    return rep // CORES, lax.rem(dom, NY), dom // NY, lax.rem(rep, CORES)


def device(x, y, z, core):
    return (z * NY + y, x * CORES + core)


def greet(others):
    barrier = pltpu.get_barrier_semaphore()
    for other in others:
        pl.semaphore_signal(barrier, inc=1, device_id=other, device_id_type=MESH)
    return lambda: pl.semaphore_wait(barrier, len(others))


def around(position, count):
    return [lax.rem(position + step, count) for step in range(1, count)]


def product(left, right, dims):
    return lax.dot_general(left, right, (dims, ((), ())), preferred_element_type=F32)


def copy_counts(nx, nz, kernels, rounds):
    chunks = -(-kernels // CHUNK)
    return 3 * rounds + 1 + chunks * (2 + 4 * (nx - 1) + 4 * (NY - 1) + 2 * (nz - 1))


def kernel(
    nx, nz, kernels, rounds,
    feats, coords, kernel_points, weights_hbm, slots, mask_hbm, sends, cot,
    output, grad, final,
    weights, mask, pool_feats, pool_pos, own_pos, send_feats, send_pos, query, cot_pair, h, grad_summed, grad_support,
    send_grad, got_grad, support, summed, summed_pair, out_sum, partial, got_first, part, got_second,
    slab, got_z, piece, gather_z, gather_second,
    local_sem, send_sem, recv_sem,
):
    leaves, points, channels = feats.shape
    near = slots.shape[1]
    bound = sends.shape[1]
    x, y, z, core = place()
    dom = z * NY + y
    sibling = device(x, y, z, 1 - core)
    axes = {
        "x": (x, nx, lambda o: device(o, y, z, core)),
        "y": (y, NY, lambda o: device(x, o, z, core)),
        "z": (z, nz, lambda o: device(x, y, o, core)),
    }
    low = NY.bit_length() - 1
    partners = []
    for bit in range(rounds):
        if bit < low:
            side = 1 << bit
            partners.append(device(x, y + side - 2 * side * lax.rem(y // side, 2), z, core))
        else:
            side = 1 << (bit - low)
            partners.append(device(x, y, z + side - 2 * side * lax.rem(z // side, 2), core))
    others = [sibling]
    for at, count, to in axes.values():
        others += [to(o) for o in around(at, count)]
    all_here = greet(others)

    load_weights = pltpu.make_async_copy(weights_hbm, weights, local_sem.at[0])
    load_weights.start()
    load_mask = pltpu.make_async_copy(mask_hbm, mask, local_sem.at[1])
    load_mask.start()

    number = [0]
    started = []

    def push(src, dst, other):
        index = number[0]
        number[0] += 1
        copy = pltpu.make_async_remote_copy(
            src_ref=src, dst_ref=dst, send_sem=send_sem.at[index], recv_sem=recv_sem.at[index],
            device_id=other, device_id_type=MESH,
        )
        copy.start()
        started.append(copy)
        return copy

    def arrive(copies):
        for copy in copies:
            copy.wait_recv()

    positions = coords[...].astype(F32) * QUANT
    for leaf in range(leaves):
        own = positions[:, leaf * points : (leaf + 1) * points]
        both = jnp.concatenate([own, own], 1)
        own_pos[leaf] = jnp.concatenate([both, jnp.zeros((8 - 3, 2 * points), F32)], 0)
        pool_pos[leaf] = own_pos[leaf]
        pool_feats[leaf] = feats[leaf]
    for bit in range(rounds):
        for t in range(bound):
            chosen = sends[bit, t]
            send_feats[bit * bound + t] = feats[chosen]
            send_pos[bit * bound + t] = own_pos[chosen]
    all_here()
    copies_pos, copies_feats = [], []
    for bit in reversed(range(rounds)):
        entry, there = pl.ds(bit * bound, bound), pl.ds(leaves + bit * bound, bound)
        copies_pos.append(push(send_pos.at[entry], pool_pos.at[there], partners[bit]))
    for bit in reversed(range(rounds)):
        entry, there = pl.ds(bit * bound, bound), pl.ds(leaves + bit * bound, bound)
        copies_feats.append(push(send_feats.at[entry], pool_feats.at[there], partners[bit]))
    copy_cot = push(cot, cot_pair, sibling)

    rows = lax.broadcasted_iota(jnp.int32, (points, 2 * points), 0)
    lanes = lax.broadcasted_iota(jnp.int32, (points, 2 * points), 1)
    for leaf in range(leaves):
        for c in range(3):
            line = jnp.where(rows == lanes, pool_pos[leaf, c : c + 1, :], 0.0)
            query[c, leaf] = jnp.broadcast_to(jnp.sum(line, 1, keepdims=True), (points, 2 * points))

    load_weights.wait()

    def grads(k, _):
        block = product(cot[...].reshape(leaves * points, channels), weights[k], ((1,), (1,)))
        grad_summed[:, k] = block.astype(BF16).reshape(leaves, points, channels)
        return 0

    lax.fori_loop(0, kernels, grads, 0)

    load_mask.wait()
    arrive(copies_pos)
    unroll = 3 if kernels % 3 == 0 else 1

    def correlate(leaf, _):
        for pair in range(near // 2):
            first = pool_pos[slots[leaf, 2 * pair]]
            second = pool_pos[slots[leaf, 2 * pair + 1]]
            lane = lax.broadcasted_iota(jnp.int32, first.shape, 1)
            places = jnp.where(lane < points, first, second)
            apart = [places[c : c + 1, :] - query[c, leaf] for c in range(3)]
            shown = jnp.concatenate([mask[leaf, 2 * pair], mask[leaf, 2 * pair + 1]], 1).astype(F32)

            def one(step, _):
                for k in [step * unroll + u for u in range(unroll)]:
                    squared = jnp.full(shown.shape, EPSILON, F32)
                    for c in range(3):
                        difference = apart[c] - kernel_points[k, c]
                        squared = squared + difference * difference
                    weight = jnp.maximum(1.0 - squared * lax.rsqrt(squared), 0.0) * shown
                    h[leaf, k, :, pair * 2 * points : (pair + 1) * 2 * points] = weight.astype(BF16)
                return 0

            lax.fori_loop(0, kernels // unroll, one, 0)
        return 0

    lax.fori_loop(0, leaves, correlate, 0)

    def supports(leaf, _):
        left = h[leaf].reshape(kernels * points, near * points)
        right = grad_summed[leaf].reshape(kernels * points, channels)
        grad_support[leaf] = product(left, right, ((0,), (0,)))
        return 0

    lax.fori_loop(0, leaves, supports, 0)

    def gathered(entry, total):
        for leaf in range(leaves):
            for n in range(1, near):
                named = jnp.where(slots[leaf, n] == entry, 1.0, 0.0)
                total = total + named * grad_support[leaf, n * points : (n + 1) * points, :]
        return total

    def away(entry, _):
        send_grad[entry] = gathered(entry + leaves, jnp.zeros((points, channels), F32)).astype(BF16)
        return 0

    lax.fori_loop(0, rounds * bound, away, 0)
    copies_grad = []
    for bit in reversed(range(rounds)):
        entry = pl.ds(bit * bound, bound)
        copies_grad.append(push(send_grad.at[entry], got_grad.at[entry], partners[bit]))

    half = channels // CORES
    own_half = pl.ds(pl.multiple_of(core * half, half), half)
    pair_half = pl.ds(pl.multiple_of((1 - core) * half, half), half)
    chunks = [(k0, min(CHUNK, kernels - k0)) for k0 in range(0, kernels, CHUNK)]
    arrive(copies_feats)
    for leaf in range(leaves):
        for n in range(near):
            support[leaf, n * points : (n + 1) * points, :] = pool_feats[slots[leaf, n]]
    copies_summed = []
    for k0, nk in chunks:

        def sums(leaf, _, k0=k0, nk=nk):
            left = h[leaf, k0 : k0 + nk].reshape(nk * points, near * points)
            block = product(left, support[leaf], ((1,), (0,))).astype(BF16)
            at = pl.ds(pl.multiple_of(leaf * points, points), points)
            summed[k0 : k0 + nk, at, :] = block.reshape(nk, points, channels)
            return 0

        lax.fori_loop(0, leaves, sums, 0)
        there = pl.ds(k0, nk)
        copies_summed.append(push(summed.at[there, :, pair_half], summed_pair.at[there], sibling))

    arrive([copy_cot])
    groups = []
    for k0, nk in chunks:
        cut = min(CHUNK // 2, nk)
        groups.append([(k0, cut, "x", "y"), (k0 + cut, nk - cut, "y", "x")])

    def band(axis, at):
        block = half // axes[axis][1]
        return pl.ds(pl.multiple_of(at * block, block), block)

    def tile(axis, at):
        block = part.shape[1] // (axes[axis][1] // 2)
        width = channels // 2
        down, across = at // 2, lax.rem(at, 2)
        return pl.ds(pl.multiple_of(down * block, block), block), pl.ds(pl.multiple_of(across * width, width), width)

    firsts = []
    for (k0, nk), copy, pieces in zip(chunks, copies_summed, groups):
        arrive([copy])

        def terms(k, _):
            block = product(summed[k, :, own_half], cot[...].reshape(leaves * points, channels), ((0,), (0,)))
            block += product(summed_pair[k], cot_pair[...].reshape(leaves * points, channels), ((0,), (0,)))
            partial[k] = block.astype(BF16)
            return 0

        sent = []
        for g0, ng, first, _ in pieces:
            lax.fori_loop(g0, g0 + ng, terms, 0)
            at, count, to = axes[first]
            there = pl.ds(g0, ng)
            sent.append([
                push(partial.at[there, band(first, o), :], got_first.at[step, there], to(o))
                for step, o in enumerate(around(at, count))
            ])
        firsts.append(sent)

    out_sum[...] = jnp.zeros(out_sum.shape, F32)

    def outputs(k, _):
        out_sum[...] += product(summed[k], weights[k], ((1,), (0,)))
        return 0

    lax.fori_loop(0, kernels, outputs, 0)
    output[...] = out_sum[...].astype(BF16).reshape(output.shape)

    seconds = []
    for sent, pieces in zip(firsts, groups):
        again = []
        for copies, (g0, ng, first, second) in zip(sent, pieces):
            arrive(copies)
            at, count, _ = axes[first]
            own = band(first, at)

            def add_first(k, _, own=own, count=count):
                total = partial[k, own, :].astype(F32)
                for step in range(count - 1):
                    total = total + got_first[step, k].astype(F32)
                part[k] = total.astype(BF16)
                return 0

            lax.fori_loop(g0, g0 + ng, add_first, 0)
            at, count, to = axes[second]
            there = pl.ds(g0, ng)
            again.append([
                push(part.at[there, *tile(second, o)], got_second.at[step, there], to(o))
                for step, o in enumerate(around(at, count))
            ])
        seconds.append(again)

    arrive(copies_grad)

    def owned(leaf, _):
        total = gathered(leaf, grad_support[leaf, 0:points, :])
        for bit in range(rounds):
            for t in range(bound):
                named = jnp.where(sends[bit, t] == leaf, 1.0, 0.0)
                total = total + named * got_grad[bit * bound + t].astype(F32)
        grad[leaf] = total.astype(BF16)
        return 0

    lax.fori_loop(0, leaves, owned, 0)

    per_z = CHUNK // nz
    for k in range(kernels, slab.shape[0]):
        slab[k] = jnp.zeros(slab.shape[1:], BF16)
    thirds = []
    for index, (again, pieces) in enumerate(zip(seconds, groups)):
        for copies, (g0, ng, _, second) in zip(again, pieces):
            arrive(copies)
            at, count, _ = axes[second]
            own = tile(second, at)

            def add_second(k, _, own=own, count=count):
                total = part[k, own[0], own[1]].astype(F32)
                for step in range(count - 1):
                    total = total + got_second[step, k].astype(F32)
                slab[k] = total.astype(BF16)
                return 0

            lax.fori_loop(g0, g0 + ng, add_second, 0)
        at, count, to = axes["z"]
        thirds.append([
            push(slab.at[pl.ds(index * CHUNK + o * per_z, per_z)], got_z.at[index, step], to(o))
            for step, o in enumerate(around(at, count))
        ])
    back_z = []
    for index, copies in enumerate(thirds):
        arrive(copies)
        at, count, to = axes["z"]
        own = pl.ds(index * CHUNK + z * per_z, per_z)
        total = slab[own].astype(F32)
        for step in range(count - 1):
            total = total + got_z[index, step].astype(F32)
        piece[index] = (total / (nx * NY * nz * CORES)).astype(BF16)
        back_z.append([push(piece.at[index], gather_z.at[own], to(o)) for o in around(at, count)])
        gather_z[own] = piece[index]
    back_second = []
    for copies, pieces in zip(back_z, groups):
        arrive(copies)
        sent = []
        for g0, ng, _, second in pieces:
            at, count, to = axes[second]
            there = pl.ds(g0, ng)
            own = tile(second, at)
            sent.append([
                push(gather_z.at[there], gather_second.at[there, *own], to(o)) for o in around(at, count)
            ])
            gather_second[there, own[0], own[1]] = gather_z[there]
        back_second.append(sent)
    back_first = []
    for sent, pieces in zip(back_second, groups):
        again = []
        for copies, (g0, ng, first, _) in zip(sent, pieces):
            arrive(copies)
            at, count, to = axes[first]
            there = pl.ds(g0, ng)
            block = half // count
            own = pl.ds(pl.multiple_of(core * half + at * block, block), block)
            again.append([
                push(gather_second.at[there], final.at[there, own, :], to(o)) for o in around(at, count)
            ])
            final[there, own, :] = gather_second[there]
        back_first.append(again)
    lasts = []
    for again, (k0, nk) in zip(back_first, chunks):
        for copies in again:
            arrive(copies)
        mine = final.at[pl.ds(k0, nk), own_half, :]
        lasts.append(push(mine, mine, sibling))
    arrive(lasts)
    for copy in started:
        copy.wait_send()


def shards(features, coords, kernel_points, weights, support_slot, slot_mask, send_leaf, cotangent):
    leaves, points, channels = features.shape[1:]
    kernels = kernel_points.shape[0]
    near = support_slot.shape[2]
    nx, nz = lax.axis_size("rep") // CORES, lax.axis_size("dom") // NY
    rounds = lax.axis_size("dom").bit_length() - 1
    bound = send_leaf.shape[3]
    received = rounds * bound
    chunks = -(-kernels // CHUNK)
    padded = chunks * CHUNK
    half = channels // CORES
    wide = max(nx, NY)
    band = half // min(nx, NY)
    tile = band // (wide // 2)
    width = channels // 2
    copies = copy_counts(nx, nz, kernels, rounds)
    vmem, smem, anywhere = (
        pl.BlockSpec(memory_space=space) for space in (pltpu.VMEM, pltpu.SMEM, pl.ANY)
    )
    cube = (kernels, channels, channels)
    leaf_shape = (leaves, points, channels)
    output, grad, mean = pl.pallas_call(
        functools.partial(kernel, nx, nz, kernels, rounds),
        out_shape=(
            jax.ShapeDtypeStruct(leaf_shape, BF16),
            jax.ShapeDtypeStruct(leaf_shape, BF16),
            jax.ShapeDtypeStruct(cube, BF16),
        ),
        in_specs=[vmem, vmem, smem, anywhere, smem, anywhere, smem, vmem],
        out_specs=(vmem, vmem, vmem),
        scratch_shapes=[
            pltpu.VMEM(cube, BF16),
            pltpu.VMEM(slot_mask.shape[1:], jnp.int32),
            pltpu.VMEM((leaves + received, points, channels), BF16),
            pltpu.VMEM((leaves + received, 8, 2 * points), F32),
            pltpu.VMEM((leaves, 8, 2 * points), F32),
            pltpu.VMEM((received, points, channels), BF16),
            pltpu.VMEM((received, 8, 2 * points), F32),
            pltpu.VMEM((3, leaves, points, 2 * points), F32),
            pltpu.VMEM(leaf_shape, BF16),
            pltpu.VMEM((leaves, kernels, points, near * points), BF16),
            pltpu.VMEM((leaves, kernels, points, channels), BF16),
            pltpu.VMEM((leaves, near * points, channels), F32),
            pltpu.VMEM((received, points, channels), BF16),
            pltpu.VMEM((received, points, channels), BF16),
            pltpu.VMEM((leaves, near * points, channels), BF16),
            pltpu.VMEM((kernels, leaves * points, channels), BF16),
            pltpu.VMEM((kernels, leaves * points, half), BF16),
            pltpu.VMEM((leaves * points, channels), F32),
            pltpu.VMEM((kernels, half, channels), BF16),
            pltpu.VMEM((wide - 1, kernels, band, channels), BF16),
            pltpu.VMEM((kernels, band, channels), BF16),
            pltpu.VMEM((wide - 1, kernels, tile, width), BF16),
            pltpu.VMEM((padded, tile, width), BF16),
            pltpu.VMEM((chunks, nz - 1, CHUNK // nz, tile, width), BF16),
            pltpu.VMEM((chunks, CHUNK // nz, tile, width), BF16),
            pltpu.VMEM((padded, tile, width), BF16),
            pltpu.VMEM((kernels, band, channels), BF16),
            pltpu.SemaphoreType.DMA((2,)),
            pltpu.SemaphoreType.DMA((copies,)),
            pltpu.SemaphoreType.DMA((copies,)),
        ],
        compiler_params=pltpu.CompilerParams(
            collective_id=0, has_side_effects=True, vmem_limit_bytes=48 * 1024 * 1024
        ),
        name="convolution",
    )(
        features[0], coords[0], kernel_points, weights.reshape(cube), support_slot[0], slot_mask[0],
        send_leaf[0, 0], cotangent[0],
    )
    grad_weight = mean.astype(F32).reshape(kernels * channels, channels)
    return (output[None], grad[None], grad_weight)


def solution(mesh):
    in_specs = (
        P("rep", "dom", None, None),
        P("rep", None, "dom"),
        P(),
        P(),
        P("rep", "dom", None),
        P("rep", "dom", None, None, None),
        P("rep", "dom", None, None),
        P("rep", "dom", None, None),
    )
    out_specs = (P("rep", "dom", None, None), P("rep", "dom", None, None), P())
    return jax.shard_map(shards, mesh=mesh, in_specs=in_specs, out_specs=out_specs, check_vma=False)
```

```python
import functools

import jax
import jax.numpy as jnp
from jax import lax
from jax.experimental import pallas as pl
from jax.experimental.pallas import tpu as pltpu
from jax.sharding import PartitionSpec as P

QUANT = 0.0625
EPSILON = 1e-06
CORES = 2
NY = 4
CHUNK = 8
MESH = pl.DeviceIdType.MESH
F32, BF16 = jnp.float32, jnp.bfloat16


def place():
    dom, rep = lax.axis_index("dom"), lax.axis_index("rep")
    return rep // CORES, lax.rem(dom, NY), dom // NY, lax.rem(rep, CORES)


def device(x, y, z, core):
    return (z * NY + y, x * CORES + core)


def greet(others):
    barrier = pltpu.get_barrier_semaphore()
    for other in others:
        pl.semaphore_signal(barrier, inc=1, device_id=other, device_id_type=MESH)
    return lambda: pl.semaphore_wait(barrier, len(others))


def steps_of(count):
    return sorted(range(1, count), key=lambda step: -min(step, count - step))


def around(position, count):
    return [lax.rem(position + step, count) for step in steps_of(count)]


def product(left, right, dims):
    return lax.dot_general(left, right, (dims, ((), ())), preferred_element_type=F32)


def copy_counts(nx, nz, kernels, rounds):
    chunks = -(-kernels // CHUNK)
    return 3 * rounds + 1 + chunks * (2 + 4 * (nx - 1) + 4 * (NY - 1) + 2 * (nz - 1) + nx + NY)


def kernel(
    nx, nz, kernels, rounds,
    feats_in, coords_in, kernel_points_in, weights_in, slots_in, mask_in, sends_in, cot_in,
    output, grad, final,
    feats, coords, kernel_points, weights, slots, mask, sends, cot, pool_feats, pool_pos, own_pos, send_feats, send_pos, query, cot_pair, h, grad_summed, grad_support,
    send_grad, got_grad, support, summed, summed_pair, partial, got_first, part, got_second,
    slab, got_z, piece, gather_z, gather_second,
    local_sem, send_sem, recv_sem,
):
    leaves, points, channels = feats.shape
    near = slots.shape[1]
    bound = sends.shape[0]
    x, y, z, core = place()
    dom = z * NY + y
    sibling = device(x, y, z, 1 - core)
    axes = {
        "x": (x, nx, lambda o: device(o, y, z, core)),
        "y": (y, NY, lambda o: device(x, o, z, core)),
        "z": (z, nz, lambda o: device(x, y, o, core)),
    }
    low = NY.bit_length() - 1
    partners = []
    for bit in range(rounds):
        if bit < low:
            side = 1 << bit
            partners.append(device(x, y + side - 2 * side * lax.rem(y // side, 2), z, core))
        else:
            side = 1 << (bit - low)
            partners.append(device(x, y, z + side - 2 * side * lax.rem(z // side, 2), core))
    others = [sibling]
    for at, count, to in axes.values():
        others += [to(o) for o in around(at, count)]
    all_here = greet(others)

    loads = {}
    for index, (name, src, dst) in enumerate((
        ("sends", sends_in, sends), ("coords", coords_in, coords), ("feats", feats_in, feats),
        ("cot", cot_in, cot), ("slots", slots_in, slots), ("points", kernel_points_in, kernel_points),
        ("weights", weights_in, weights), ("mask", mask_in, mask),
    )):
        loads[name] = pltpu.make_async_copy(src, dst, local_sem.at[index])
        loads[name].start()

    number = [0]
    started = []

    def push(src, dst, other):
        index = number[0]
        number[0] += 1
        copy = pltpu.make_async_remote_copy(
            src_ref=src, dst_ref=dst, send_sem=send_sem.at[index], recv_sem=recv_sem.at[index],
            device_id=other, device_id_type=MESH,
        )
        copy.start()
        started.append(copy)
        return copy

    def arrive(copies):
        for copy in copies:
            copy.wait_recv()

    for name in ("sends", "coords", "feats"):
        loads[name].wait()
    positions = coords[...].reshape(3, leaves * points).astype(F32) * QUANT
    for leaf in range(leaves):
        own = positions[:, leaf * points : (leaf + 1) * points]
        both = jnp.concatenate([own, own], 1)
        own_pos[leaf] = jnp.concatenate([both, jnp.zeros((8 - 3, 2 * points), F32)], 0)
        pool_pos[leaf] = own_pos[leaf]
        pool_feats[leaf] = feats[leaf]
    for bit in range(rounds):
        for t in range(bound):
            chosen = sends[t, bit]
            send_feats[bit * bound + t] = feats[chosen]
            send_pos[bit * bound + t] = own_pos[chosen]
    all_here()
    copies_pos, copies_feats = [], []
    for bit in reversed(range(rounds)):
        entry, there = pl.ds(bit * bound, bound), pl.ds(leaves + bit * bound, bound)
        copies_pos.append(push(send_pos.at[entry], pool_pos.at[there], partners[bit]))
    for bit in reversed(range(rounds)):
        entry, there = pl.ds(bit * bound, bound), pl.ds(leaves + bit * bound, bound)
        copies_feats.append(push(send_feats.at[entry], pool_feats.at[there], partners[bit]))
    loads["cot"].wait()
    copy_cot = push(cot, cot_pair, sibling)

    rows = lax.broadcasted_iota(jnp.int32, (points, 2 * points), 0)
    lanes = lax.broadcasted_iota(jnp.int32, (points, 2 * points), 1)
    for leaf in range(leaves):
        for c in range(3):
            line = jnp.where(rows == lanes, pool_pos[leaf, c : c + 1, :], 0.0)
            query[c, leaf] = jnp.broadcast_to(jnp.sum(line, 1, keepdims=True), (points, 2 * points))

    loads["weights"].wait()

    upstream = cot[...].reshape(leaves * points, channels)
    for k in range(kernels):
        block = product(upstream, weights[k], ((1,), (1,)))
        grad_summed[:, k] = block.astype(BF16).reshape(leaves, points, channels)

    for name in ("slots", "points", "mask"):
        loads[name].wait()
    arrive(copies_pos)

    def correlate(leaf, _):
        for pair in range(near // 2):
            first = pool_pos[slots[leaf, 2 * pair]]
            second = pool_pos[slots[leaf, 2 * pair + 1]]
            lane = lax.broadcasted_iota(jnp.int32, first.shape, 1)
            places = jnp.where(lane < points, first, second)
            apart = [places[c : c + 1, :] - query[c, leaf] for c in range(3)]
            shown = jnp.concatenate([mask[leaf, 2 * pair], mask[leaf, 2 * pair + 1]], 1).astype(F32)

            for k in range(kernels):
                squared = jnp.full(shown.shape, EPSILON, F32)
                for c in range(3):
                    difference = apart[c] - kernel_points[c, k]
                    squared = squared + difference * difference
                weight = jnp.maximum(1.0 - squared * lax.rsqrt(squared), 0.0) * shown
                h[leaf, k, :, pair * 2 * points : (pair + 1) * 2 * points] = weight.astype(BF16)
        return 0

    lax.fori_loop(0, leaves, correlate, 0)

    half = channels // CORES
    own_half = pl.ds(pl.multiple_of(core * half, half), half)
    pair_half = pl.ds(pl.multiple_of((1 - core) * half, half), half)
    chunks = [(k0, min(CHUNK, kernels - k0)) for k0 in range(0, kernels, CHUNK)]
    groups = []
    for k0, nk in chunks:
        cut = min(CHUNK // 2, nk)
        groups.append([(k0, cut, "x", "y"), (k0 + cut, nk - cut, "y", "x")])
    arrive(copies_feats)
    for leaf in range(leaves):
        for n in range(near):
            support[leaf, n * points : (n + 1) * points, :] = pool_feats[slots[leaf, n]]
    copies_summed = []
    for g0, ng, _, _ in sum(groups, []):
        for leaf in range(leaves):
            left = h[leaf, g0 : g0 + ng].reshape(ng * points, near * points)
            block = product(left, support[leaf], ((1,), (0,))).astype(BF16)
            summed[g0 : g0 + ng, leaf * points : (leaf + 1) * points, :] = block.reshape(ng, points, channels)
        there = pl.ds(g0, ng)
        copies_summed.append(push(summed.at[there, :, pair_half], summed_pair.at[there], sibling))

    for leaf in range(leaves):
        left = h[leaf].reshape(kernels * points, near * points)
        right = grad_summed[leaf].reshape(kernels * points, channels)
        grad_support[leaf] = product(left, right, ((0,), (0,)))

    arrive([copy_cot])

    def band(axis, at):
        block = half // axes[axis][1]
        return pl.ds(pl.multiple_of(at * block, block), block)

    def tile(axis, at):
        block = part.shape[1] // (axes[axis][1] // 2)
        width = channels // 2
        down, across = at // 2, lax.rem(at, 2)
        return pl.ds(pl.multiple_of(down * block, block), block), pl.ds(pl.multiple_of(across * width, width), width)

    upstream_pair = cot_pair[...].reshape(leaves * points, channels)
    firsts = []
    for pieces in groups:
        sent = []
        for g0, ng, first, _ in pieces:
            arrive([copies_summed.pop(0)])
            for k in range(g0, g0 + ng):
                block = product(summed[k, :, own_half].T, upstream, ((1,), (0,)))
                block += product(summed_pair[k].T, upstream_pair, ((1,), (0,)))
                partial[k] = block.astype(BF16)
            there = pl.ds(g0, ng)
            at, count, to = axes[first]
            sent.append([
                push(partial.at[there, band(first, o), :], got_first.at[step, there], to(o))
                for step, o in enumerate(around(at, count))
            ])
        firsts.append(sent)

    def gathered(entry, total):
        for leaf in range(leaves):
            for n in range(1, near):
                named = jnp.where(slots[leaf, n] == entry, 1.0, 0.0)
                total = total + named * grad_support[leaf, n * points : (n + 1) * points, :]
        return total

    def away(entry, _):
        send_grad[entry] = gathered(entry + leaves, jnp.zeros((points, channels), F32)).astype(BF16)
        return 0

    lax.fori_loop(0, rounds * bound, away, 0)
    copies_grad = []

    def hand_back(bits):
        for bit in reversed(bits):
            entry = pl.ds(bit * bound, bound)
            copies_grad.append(push(send_grad.at[entry], got_grad.at[entry], partners[bit]))

    hand_back(range(low, rounds))

    total = product(summed[0], weights[0], ((1,), (0,)))
    for k in range(1, kernels):
        total = total + product(summed[k], weights[k], ((1,), (0,)))
    output[...] = total.astype(BF16).reshape(output.shape)
    seconds = []
    for sent, pieces in zip(firsts, groups):
        again = []
        for copies, (g0, ng, first, second) in zip(sent, pieces):
            arrive(copies)
            at, count, _ = axes[first]
            own = band(first, at)

            def add_first(k, _, own=own, count=count):
                total = partial[k, own, :].astype(F32)
                for step in range(count - 1):
                    total = total + got_first[step, k].astype(F32)
                part[k] = total.astype(BF16)
                return 0

            lax.fori_loop(g0, g0 + ng, add_first, 0)
            at, count, to = axes[second]
            there = pl.ds(g0, ng)
            again.append([
                push(part.at[there, *tile(second, o)], got_second.at[step, there], to(o))
                for step, o in enumerate(around(at, count))
            ])
        seconds.append(again)

    hand_back(range(low))

    per_z = CHUNK // nz
    for k in range(kernels, slab.shape[0]):
        slab[k] = jnp.zeros(slab.shape[1:], BF16)
    thirds = []
    for index, (again, pieces) in enumerate(zip(seconds, groups)):
        for copies, (g0, ng, _, second) in zip(again, pieces):
            arrive(copies)
            at, count, _ = axes[second]
            own = tile(second, at)

            def add_second(k, _, own=own, count=count):
                total = part[k, own[0], own[1]].astype(F32)
                for step in range(count - 1):
                    total = total + got_second[step, k].astype(F32)
                slab[k] = total.astype(BF16)
                return 0

            lax.fori_loop(g0, g0 + ng, add_second, 0)
        at, count, to = axes["z"]
        thirds.append([
            push(slab.at[pl.ds(index * CHUNK + o * per_z, per_z)], got_z.at[index, step], to(o))
            for step, o in enumerate(around(at, count))
        ])
    back_z = []
    for index, copies in enumerate(thirds):
        arrive(copies)
        at, count, to = axes["z"]
        own = pl.ds(index * CHUNK + z * per_z, per_z)
        total = slab[own].astype(F32)
        for step in range(count - 1):
            total = total + got_z[index, step].astype(F32)
        piece[index] = (total / (nx * NY * nz * CORES)).astype(BF16)
        back_z.append([push(piece.at[index], gather_z.at[own], to(o)) for o in around(at, count)])
        gather_z[own] = piece[index]
    arrive(copies_grad)

    def owned(leaf, _):
        total = gathered(leaf, grad_support[leaf, 0:points, :])
        for bit in range(rounds):
            for t in range(bound):
                named = jnp.where(sends[t, bit] == leaf, 1.0, 0.0)
                total = total + named * got_grad[bit * bound + t].astype(F32)
        grad[leaf] = total.astype(BF16)
        return 0

    lax.fori_loop(0, leaves, owned, 0)

    back_second = []
    for copies, pieces in zip(back_z, groups):
        arrive(copies)
        sent = []
        for g0, ng, _, second in pieces:
            at, count, to = axes[second]
            there = pl.ds(g0, ng)
            own = tile(second, at)
            sent.append([
                push(gather_z.at[there], gather_second.at[there, *own], to(o)) for o in around(at, count)
            ])
            gather_second[there, own[0], own[1]] = gather_z[there]
        back_second.append(sent)
    back_first = []
    lasts = []

    def front(first, at):
        block = half // axes[first][1]
        return pl.ds(pl.multiple_of(core * half + at * block, block), block)

    def share(there, own):
        lasts.append(push(final.at[there, own, :], final.at[there, own, :], sibling))

    for sent, pieces in zip(back_second, groups):
        for copies, (g0, ng, first, _) in zip(sent, pieces):
            arrive(copies)
            at, count, to = axes[first]
            there = pl.ds(g0, ng)
            own = front(first, at)
            back_first.append([
                push(gather_second.at[there], final.at[there, own, :], to(o)) for o in around(at, count)
            ])
            final[there, own, :] = gather_second[there]
            share(there, own)
    for copies, (g0, ng, first, _) in zip(back_first, sum(groups, [])):
        at, count, _ = axes[first]
        for copy, step in reversed(list(zip(copies, steps_of(count)))):
            arrive([copy])
            share(pl.ds(g0, ng), front(first, lax.rem(at + count - step, count)))
    arrive(lasts)
    for copy in started:
        copy.wait_send()


def write_kernel(output, grad, mean, output_out, grad_out, mean_out, wide, sem):
    copies = []
    for index, (src, dst) in enumerate(((output, output_out), (grad, grad_out))):
        copies.append(pltpu.make_async_copy(src, dst, sem.at[index]))
        copies[-1].start()
    for k in range(mean.shape[0]):
        wide[k] = mean[k].astype(F32)
        copies.append(pltpu.make_async_copy(wide.at[k], mean_out.at[k], sem.at[2 + k]))
        copies[-1].start()
    for copy in copies:
        copy.wait()


def shards(features, coords, kernel_points, weights, support_slot, slot_mask, send_leaf, cotangent):
    leaves, points, channels = features.shape[1:]
    kernels = kernel_points.shape[0]
    near = support_slot.shape[2]
    nx, nz = lax.axis_size("rep") // CORES, lax.axis_size("dom") // NY
    rounds = lax.axis_size("dom").bit_length() - 1
    bound = send_leaf.shape[3]
    received = rounds * bound
    chunks = -(-kernels // CHUNK)
    padded = chunks * CHUNK
    half = channels // CORES
    wide = max(nx, NY)
    band = half // min(nx, NY)
    tile = band // (wide // 2)
    width = channels // 2
    copies = copy_counts(nx, nz, kernels, rounds)
    vmem, hbm = (pl.BlockSpec(memory_space=space) for space in (pltpu.VMEM, pltpu.HBM))
    cube = (kernels, channels, channels)
    leaf_shape = (leaves, points, channels)
    output, grad, mean = pl.pallas_call(
        functools.partial(kernel, nx, nz, kernels, rounds),
        out_shape=(
            jax.ShapeDtypeStruct(leaf_shape, BF16),
            jax.ShapeDtypeStruct(leaf_shape, BF16),
            jax.ShapeDtypeStruct(cube, BF16),
        ),
        in_specs=[hbm] * 8,
        out_specs=(vmem, vmem, vmem),
        scratch_shapes=[
            pltpu.VMEM(leaf_shape, BF16),
            pltpu.VMEM((3, 1, leaves * points), jnp.int32),
            pltpu.SMEM((3, kernels), F32),
            pltpu.VMEM(cube, BF16),
            pltpu.SMEM((leaves, near), jnp.int32),
            pltpu.VMEM(slot_mask.shape[1:], jnp.int32),
            pltpu.SMEM((bound, rounds), jnp.int32),
            pltpu.VMEM(leaf_shape, BF16),
            pltpu.VMEM((leaves + received, points, channels), BF16),
            pltpu.VMEM((leaves + received, 8, 2 * points), F32),
            pltpu.VMEM((leaves, 8, 2 * points), F32),
            pltpu.VMEM((received, points, channels), BF16),
            pltpu.VMEM((received, 8, 2 * points), F32),
            pltpu.VMEM((3, leaves, points, 2 * points), F32),
            pltpu.VMEM(leaf_shape, BF16),
            pltpu.VMEM((leaves, kernels, points, near * points), BF16),
            pltpu.VMEM((leaves, kernels, points, channels), BF16),
            pltpu.VMEM((leaves, near * points, channels), F32),
            pltpu.VMEM((received, points, channels), BF16),
            pltpu.VMEM((received, points, channels), BF16),
            pltpu.VMEM((leaves, near * points, channels), BF16),
            pltpu.VMEM((kernels, leaves * points, channels), BF16),
            pltpu.VMEM((kernels, leaves * points, half), BF16),
            pltpu.VMEM((kernels, half, channels), BF16),
            pltpu.VMEM((wide - 1, kernels, band, channels), BF16),
            pltpu.VMEM((kernels, band, channels), BF16),
            pltpu.VMEM((wide - 1, kernels, tile, width), BF16),
            pltpu.VMEM((padded, tile, width), BF16),
            pltpu.VMEM((chunks, nz - 1, CHUNK // nz, tile, width), BF16),
            pltpu.VMEM((chunks, CHUNK // nz, tile, width), BF16),
            pltpu.VMEM((padded, tile, width), BF16),
            pltpu.VMEM((kernels, band, channels), BF16),
            pltpu.SemaphoreType.DMA((8,)),
            pltpu.SemaphoreType.DMA((copies,)),
            pltpu.SemaphoreType.DMA((copies,)),
        ],
        compiler_params=pltpu.CompilerParams(
            collective_id=0, has_side_effects=True, vmem_limit_bytes=48 * 1024 * 1024
        ),
        name="convolution",
    )(
        *(
            pltpu.with_memory_space_constraint(operand, pltpu.HBM)
            for operand in (
                features[0], coords.transpose(1, 0, 2), kernel_points.T, weights.reshape(cube), support_slot[0],
                slot_mask[0], send_leaf[0, 0].T, cotangent[0],
            )
        )
    )
    output, grad, grad_weight = pl.pallas_call(
        write_kernel,
        out_shape=(
            jax.ShapeDtypeStruct(leaf_shape, BF16),
            jax.ShapeDtypeStruct(leaf_shape, BF16),
            jax.ShapeDtypeStruct(cube, F32),
        ),
        in_specs=[vmem, vmem, vmem],
        out_specs=(hbm, hbm, hbm),
        scratch_shapes=[pltpu.VMEM(cube, F32), pltpu.SemaphoreType.DMA((2 + kernels,))],
        compiler_params=pltpu.CompilerParams(vmem_limit_bytes=16 * 1024 * 1024),
        name="write",
    )(output, grad, mean)
    return (output[None], grad[None], grad_weight.reshape(kernels * channels, channels))


def solution(mesh):
    in_specs = (
        P("rep", "dom", None, None),
        P("rep", None, "dom"),
        P(),
        P(),
        P("rep", "dom", None),
        P("rep", "dom", None, None, None),
        P("rep", "dom", None, None),
        P("rep", "dom", None, None),
    )
    out_specs = (P("rep", "dom", None, None), P("rep", "dom", None, None), P())
    return jax.shard_map(shards, mesh=mesh, in_specs=in_specs, out_specs=out_specs, check_vma=False)
```

```python
import functools

import jax
import jax.numpy as jnp
from jax import lax
from jax.experimental import pallas as pl
from jax.experimental.pallas import tpu as pltpu
from jax.sharding import PartitionSpec as P

QUANT = 0.0625
EPSILON = 1e-06
CORES = 2
NY = 4
CHUNK = 8
CHUNKS = 2
MESH = pl.DeviceIdType.MESH
F32, BF16 = jnp.float32, jnp.bfloat16


def place():
    dom, rep = lax.axis_index("dom"), lax.axis_index("rep")
    return rep // CORES, lax.rem(dom, NY), dom // NY, lax.rem(rep, CORES)


def device(x, y, z, core):
    return (z * NY + y, x * CORES + core)


def greet(others):
    barrier = pltpu.get_barrier_semaphore()
    for other in others:
        pl.semaphore_signal(barrier, inc=1, device_id=other, device_id_type=MESH)


def all_here(count):
    pl.semaphore_wait(pltpu.get_barrier_semaphore(), count)


def steps_of(count):
    return sorted(range(1, count), key=lambda step: -min(step, count - step))


def around(position, count):
    return [lax.rem(position + step, count) for step in steps_of(count)]


def product(left, right, dims):
    return lax.dot_general(left, right, (dims, ((), ())), preferred_element_type=F32)


def copy_counts(nx, nz, rounds):
    return 3 * rounds + 1 + CHUNKS * (2 + 6 * (nx - 1 + NY - 1) + 4 + 2 * (nz - 1) + nx + NY)


def kernel(
    nx, nz, kernels, rounds,
    feats_in, coords_in, kernel_points_in, weights_in, slots_in, mask_in, sends_in, cot_in,
    output, grad, final,
    feats, coords, kernel_points, weights, slots, mask, sends, cot, pool_feats, pool_pos, own_pos, send_feats, send_pos, query, cot_pair, h, grad_summed, grad_support,
    send_grad, got_grad, support, summed, summed_pair, partial, partial_pair, got_first, part, got_second,
    slab, got_z, piece, gather_z, gather_second,
    local_sem, send_sem, recv_sem,
):
    leaves, points, channels = feats.shape
    near = slots.shape[1]
    bound = sends.shape[0]
    x, y, z, core = place()
    dom = z * NY + y
    sibling = device(x, y, z, 1 - core)
    axes = {
        "x": (x, nx, lambda o, c: device(o, y, z, c)),
        "y": (y, NY, lambda o, c: device(x, o, z, c)),
        "z": (z, nz, lambda o, c: device(x, y, o, c)),
    }
    low = NY.bit_length() - 1
    partners = []
    for bit in range(rounds):
        if bit < low:
            side = 1 << bit
            partners.append(device(x, y + side - 2 * side * lax.rem(y // side, 2), z, core))
        else:
            side = 1 << (bit - low)
            partners.append(device(x, y, z + side - 2 * side * lax.rem(z // side, 2), core))
    rings = {axis: [(to, o) for o in around(at, count)] for axis, (at, count, to) in axes.items()}
    plane = rings["x"] + rings["y"]

    @pl.when(core == 1)
    def _():
        greet([sibling] + [to(o, 1) for to, o in plane + rings["z"]] + [to(o, 0) for to, o in plane])

    @pl.when(core == 0)
    def _():
        greet([sibling] + partners + [to(o, 1) for to, o in plane])

    loads = {}
    for index, (name, src, dst) in enumerate((
        ("sends", sends_in, sends), ("coords", coords_in, coords), ("feats", feats_in, feats),
        ("cot", cot_in, cot), ("slots", slots_in, slots), ("points", kernel_points_in, kernel_points),
        ("weights", weights_in, weights), ("mask", mask_in, mask),
    )):
        loads[name] = pltpu.make_async_copy(src, dst, local_sem.at[index])
        loads[name].start()

    number = [0]
    started = []
    settled = [0]

    def describe(src, dst, other):
        index = number[0]
        number[0] += 1
        return pltpu.make_async_remote_copy(
            src_ref=src, dst_ref=dst, send_sem=send_sem.at[index], recv_sem=recv_sem.at[index],
            device_id=other, device_id_type=MESH,
        )

    def push(src, dst, other):
        return begin(describe(src, dst, other))

    def begin(copy):
        copy.start()
        started.append(copy)
        return copy

    def arrive(copies):
        for copy in copies:
            copy.wait_recv()

    def settle(count):
        for copy in started[settled[0] : count]:
            copy.wait_send()
        settled[0] = max(settled[0], count)

    for name in ("sends", "coords", "feats"):
        loads[name].wait()
    positions = coords[...].reshape(3, leaves * points).astype(F32) * QUANT
    for leaf in range(leaves):
        own = positions[:, leaf * points : (leaf + 1) * points]
        both = jnp.concatenate([own, own], 1)
        own_pos[leaf] = jnp.concatenate([both, jnp.zeros((8 - 3, 2 * points), F32)], 0)
        pool_pos[leaf] = own_pos[leaf]
        pool_feats[leaf] = feats[leaf]
    for bit in range(rounds):
        for t in range(bound):
            chosen = sends[t, bit]
            send_feats[bit * bound + t] = feats[chosen]
            send_pos[bit * bound + t] = own_pos[chosen]

    @pl.when(core == 1)
    def _():
        all_here(1 + 2 * len(plane) + len(rings["z"]))

    @pl.when(core == 0)
    def _():
        all_here(1 + len(partners) + len(plane))

    copies_pos, copies_feats = [], []
    for bit in reversed(range(rounds)):
        entry, there = pl.ds(bit * bound, bound), pl.ds(leaves + bit * bound, bound)
        copies_pos.append(push(send_pos.at[entry], pool_pos.at[there], partners[bit]))
    for bit in reversed(range(rounds)):
        entry, there = pl.ds(bit * bound, bound), pl.ds(leaves + bit * bound, bound)
        copies_feats.append(push(send_feats.at[entry], pool_feats.at[there], partners[bit]))
    loads["cot"].wait()
    copy_cot = push(cot, cot_pair, sibling)

    rows = lax.broadcasted_iota(jnp.int32, (points, 2 * points), 0)
    lanes = lax.broadcasted_iota(jnp.int32, (points, 2 * points), 1)
    for leaf in range(leaves):
        for c in range(3):
            line = jnp.where(rows == lanes, pool_pos[leaf, c : c + 1, :], 0.0)
            query[c, leaf] = jnp.broadcast_to(jnp.sum(line, 1, keepdims=True), (points, 2 * points))

    loads["weights"].wait()

    upstream = cot[...].reshape(leaves * points, channels)
    for k in range(kernels):
        block = product(upstream, weights[k], ((1,), (1,)))
        grad_summed[:, k] = block.astype(BF16).reshape(leaves, points, channels)

    for name in ("slots", "points", "mask"):
        loads[name].wait()
    arrive(copies_pos)

    def correlate(leaf, _):
        for pair in range(near // 2):
            first = pool_pos[slots[leaf, 2 * pair]]
            second = pool_pos[slots[leaf, 2 * pair + 1]]
            lane = lax.broadcasted_iota(jnp.int32, first.shape, 1)
            places = jnp.where(lane < points, first, second)
            apart = [places[c : c + 1, :] - query[c, leaf] for c in range(3)]
            shown = jnp.concatenate([mask[leaf, 2 * pair], mask[leaf, 2 * pair + 1]], 1).astype(F32)

            for k in range(kernels):
                squared = jnp.full(shown.shape, EPSILON, F32)
                for c in range(3):
                    difference = apart[c] - kernel_points[c, k]
                    squared = squared + difference * difference
                weight = jnp.maximum(1.0 - squared * lax.rsqrt(squared), 0.0) * shown
                h[leaf, k, :, pair * 2 * points : (pair + 1) * 2 * points] = weight.astype(BF16)
        return 0

    lax.fori_loop(0, leaves, correlate, 0)

    half = channels // CORES
    own_half = pl.ds(pl.multiple_of(core * half, half), half)
    pair_half = pl.ds(pl.multiple_of((1 - core) * half, half), half)
    chunks = [(kernels * i // CHUNKS, kernels * (i + 1) // CHUNKS - kernels * i // CHUNKS) for i in range(CHUNKS)]
    groups = []
    for k0, nk in chunks:
        cut = (nk + 1) // 2
        groups.append([(k0, cut, "x", "y"), (k0 + cut, nk - cut, "y", "x")])
    pairs = sum(groups, [])

    def band(axis, at, start=0):
        block = half // axes[axis][1]
        return pl.ds(pl.multiple_of(start + at * block, block), block)

    def tile(axis, at):
        block = part.shape[1] // axes[axis][1]
        return pl.ds(pl.multiple_of(at * block, block), block)

    firsts, fronts, lasts = {}, {}, {}
    for g0, ng, first, _ in pairs:
        there = pl.ds(g0, ng)
        at, count, to = axes[first]
        block = half // count
        for side in range(CORES):
            rows = pl.ds(side * block, block)
            for step, o in zip(steps_of(count), around(at, count)):
                firsts[g0, step, side] = describe(
                    partial.at[there, band(first, o), :], got_first.at[step - 1, there, rows, :], to(o, 1)
                )
                fronts[g0, step, side] = describe(
                    gather_second.at[there, rows, :], final.at[there, band(first, at, side * half), :], to(o, side)
                )
        firsts[g0, 0, 0] = describe(partial.at[there, band(first, at), :], partial_pair.at[there], sibling)
        fronts[g0, 0, 0] = describe(
            gather_second.at[there, pl.ds(0, block), :], final.at[there, band(first, at), :], sibling
        )
        for step in range(count):
            here = final.at[there, band(first, lax.rem(at + count - step, count), core * half), :]
            lasts[g0, step] = describe(here, here, sibling)

    arrive(copies_feats)
    for leaf in range(leaves):
        for n in range(near):
            support[leaf, n * points : (n + 1) * points, :] = pool_feats[slots[leaf, n]]
    copies_summed = []
    for g0, ng, _, _ in pairs:
        for leaf in range(leaves):
            left = h[leaf, g0 : g0 + ng].reshape(ng * points, near * points)
            block = product(left, support[leaf], ((1,), (0,))).astype(BF16)
            summed[g0 : g0 + ng, leaf * points : (leaf + 1) * points, :] = block.reshape(ng, points, channels)
        there = pl.ds(g0, ng)
        copies_summed.append(push(summed.at[there, :, pair_half], summed_pair.at[there], sibling))

    arrive([copy_cot])
    upstream_pair = cot_pair[...].reshape(leaves * points, channels)
    for copy, (g0, ng, first, _) in zip(copies_summed, pairs):
        arrive([copy])
        for k in range(g0, g0 + ng):
            block = product(summed[k, :, own_half].T, upstream, ((1,), (0,)))
            block += product(summed_pair[k].T, upstream_pair, ((1,), (0,)))
            partial[k] = block.astype(BF16)
        for side in range(CORES):

            @pl.when(core == side)
            def _():
                for step in steps_of(axes[first][1]) + [0] * (1 - side):
                    firsts[g0, step, side].start()

    def gathered(entry, total):
        for leaf in range(leaves):
            for n in range(1, near):
                named = jnp.where(slots[leaf, n] == entry, 1.0, 0.0)
                total = total + named * grad_support[leaf, n * points : (n + 1) * points, :]
        return total

    def away(entry, _):
        send_grad[entry] = gathered(entry + leaves, jnp.zeros((points, channels), F32)).astype(BF16)
        return 0

    def feature_gradients():
        for leaf in range(leaves):
            left = h[leaf].reshape(kernels * points, near * points)
            right = grad_summed[leaf].reshape(kernels * points, channels)
            grad_support[leaf] = product(left, right, ((0,), (0,)))
        lax.fori_loop(0, rounds * bound, away, 0)

    def hand_back(bits):
        copies = []
        for bit in reversed(bits):
            entry = pl.ds(bit * bound, bound)
            copies.append(push(send_grad.at[entry], got_grad.at[entry], partners[bit]))
        return copies

    def outputs():
        total = product(summed[0], weights[0], ((1,), (0,)))
        for k in range(1, kernels):
            total = total + product(summed[k], weights[k], ((1,), (0,)))
        output[...] = total.astype(BF16).reshape(output.shape)

    def owned(leaf, _):
        total = gathered(leaf, grad_support[leaf, 0:points, :])
        for bit in range(rounds):
            for t in range(bound):
                named = jnp.where(sends[t, bit] == leaf, 1.0, 0.0)
                total = total + named * got_grad[bit * bound + t].astype(F32)
        grad[leaf] = total.astype(BF16)
        return 0

    common = len(started), number[0]

    def exchange(side):
        for g0, ng, first, _ in pairs:
            for step in steps_of(axes[first][1])[::-1]:
                fronts[g0, step, side].wait_recv()
                lasts[g0, step].start()
            if side == 0:
                fronts[g0, 0, 0].wait_recv()
        for (_, step), copy in lasts.items():
            if step > 0 or side == 0:
                copy.wait_recv()
        for (_, step), copy in lasts.items():
            if step > 0 or side == 1:
                copy.wait_send()

    @pl.when(core == 0)
    def _():
        feature_gradients()
        copies = hand_back(range(rounds))
        outputs()
        arrive(copies)
        lax.fori_loop(0, leaves, owned, 0)
        settle(len(started))
        for (_, _, side), copy in firsts.items():
            if side == 0:
                copy.wait_send()
        exchange(0)

    del started[common[0] :]
    number[0], settled[0] = common[1], 0

    @pl.when(core == 1)
    def _():
        feature_gradients()
        copies_grad = hand_back(range(low, rounds))
        outputs()

        seconds = {}
        for g0, ng, first, second in pairs:
            at, count, _ = axes[first]
            block = half // count
            for step in [0] + steps_of(count)[::-1]:
                for side in range(CORES if step else 1):
                    firsts[g0, step, side].wait_recv()
            for k in range(g0, g0 + ng):
                for side, own in ((0, partial_pair[k]), (1, partial[k, band(first, at), :])):
                    rows = slice(side * block, (side + 1) * block)
                    total = own.astype(F32)
                    for step in range(count - 1):
                        total = total + got_first[step, k, rows, :].astype(F32)
                    part[k, rows, :] = total.astype(BF16)
            at, count, to = axes[second]
            there = pl.ds(g0, ng)
            seconds[g0] = [
                push(part.at[there, tile(second, o), :], got_second.at[step, there], to(o, 1))
                for step, o in enumerate(around(at, count))
            ]
        copies_grad += hand_back(range(low))

        per_z = CHUNK // nz
        early = len(started)
        thirds = []
        for index, (k0, nk) in enumerate(chunks):
            base = index * CHUNK - k0
            for k in range(k0 + nk, k0 + CHUNK):
                slab[base + k] = jnp.zeros(slab.shape[1:], BF16)
            for g0, ng, _, second in groups[index]:
                arrive(seconds[g0])
                at, count, _ = axes[second]
                for k in range(g0, g0 + ng):
                    total = part[k, tile(second, at), :].astype(F32)
                    for step in range(count - 1):
                        total = total + got_second[step, k].astype(F32)
                    slab[base + k] = total.astype(BF16)
            at, count, to = axes["z"]
            thirds.append([
                push(slab.at[pl.ds(index * CHUNK + o * per_z, per_z)], got_z.at[index, step], to(o, 1))
                for step, o in enumerate(around(at, count))
            ])
        devices = nx * NY * nz * CORES
        back_z = []
        for index, copies in enumerate(thirds):
            arrive(copies)
            at, count, to = axes["z"]
            own = pl.ds(index * CHUNK + z * per_z, per_z)
            total = slab[own].astype(F32)
            for step in range(count - 1):
                total = total + got_z[index, step].astype(F32)
            piece[index] = (total / devices).astype(BF16)
            back_z.append([push(piece.at[index], gather_z.at[own], to(o, 1)) for o in around(at, count)])
            gather_z[own] = piece[index]
        arrive(copies_grad)
        lax.fori_loop(0, leaves, owned, 0)
        settle(early)

        back_second = {}
        for index, (k0, nk) in enumerate(chunks):
            arrive(back_z[index])
            for g0, ng, _, second in groups[index]:
                at, count, to = axes[second]
                there, here = pl.ds(g0, ng), pl.ds(index * CHUNK + g0 - k0, ng)
                own = tile(second, at)
                back_second[g0] = [
                    push(gather_z.at[here], gather_second.at[there, own, :], to(o, 1)) for o in around(at, count)
                ]
                gather_second[there, own, :] = gather_z[here]
        for g0, ng, first, _ in pairs:
            arrive(back_second[g0])
            at, count, _ = axes[first]
            block = half // count
            for step in steps_of(count) + [0]:
                for side in range(CORES if step else 1):
                    fronts[g0, step, side].start()
            there = pl.ds(g0, ng)
            for side in range(CORES):
                rows = slice(side * block, (side + 1) * block)
                final[there, band(first, at, side * half), :] = gather_second[there, rows, :]
            lasts[g0, 0].start()
        settle(len(started))
        for (_, _, side), copy in firsts.items():
            if side == 1:
                copy.wait_send()
        exchange(1)
        for copy in fronts.values():
            copy.wait_send()


def write_kernel(output, grad, mean, output_out, grad_out, mean_out, wide, sem):
    copies = []
    for index, (src, dst) in enumerate(((output, output_out), (grad, grad_out))):
        copies.append(pltpu.make_async_copy(src, dst, sem.at[index]))
        copies[-1].start()
    for k in range(mean.shape[0]):
        wide[k] = mean[k].astype(F32)
        copies.append(pltpu.make_async_copy(wide.at[k], mean_out.at[k], sem.at[2 + k]))
        copies[-1].start()
    for copy in copies:
        copy.wait()


def shards(features, coords, kernel_points, weights, support_slot, slot_mask, send_leaf, cotangent):
    leaves, points, channels = features.shape[1:]
    kernels = kernel_points.shape[0]
    near = support_slot.shape[2]
    nx, nz = lax.axis_size("rep") // CORES, lax.axis_size("dom") // NY
    rounds = lax.axis_size("dom").bit_length() - 1
    bound = send_leaf.shape[3]
    received = rounds * bound
    padded = CHUNKS * CHUNK
    half = channels // CORES
    wide, narrow = max(nx, NY), min(nx, NY)
    band, tile = channels // narrow, channels // (nx * NY)
    copies = copy_counts(nx, nz, rounds)
    vmem, hbm = (pl.BlockSpec(memory_space=space) for space in (pltpu.VMEM, pltpu.HBM))
    cube = (kernels, channels, channels)
    leaf_shape = (leaves, points, channels)
    output, grad, mean = pl.pallas_call(
        functools.partial(kernel, nx, nz, kernels, rounds),
        out_shape=(
            jax.ShapeDtypeStruct(leaf_shape, BF16),
            jax.ShapeDtypeStruct(leaf_shape, BF16),
            jax.ShapeDtypeStruct(cube, BF16),
        ),
        in_specs=[hbm] * 8,
        out_specs=(vmem, vmem, vmem),
        scratch_shapes=[
            pltpu.VMEM(leaf_shape, BF16),
            pltpu.VMEM((3, 1, leaves * points), jnp.int32),
            pltpu.SMEM((3, kernels), F32),
            pltpu.VMEM(cube, BF16),
            pltpu.SMEM((leaves, near), jnp.int32),
            pltpu.VMEM(slot_mask.shape[1:], jnp.int32),
            pltpu.SMEM((bound, rounds), jnp.int32),
            pltpu.VMEM(leaf_shape, BF16),
            pltpu.VMEM((leaves + received, points, channels), BF16),
            pltpu.VMEM((leaves + received, 8, 2 * points), F32),
            pltpu.VMEM((leaves, 8, 2 * points), F32),
            pltpu.VMEM((received, points, channels), BF16),
            pltpu.VMEM((received, 8, 2 * points), F32),
            pltpu.VMEM((3, leaves, points, 2 * points), F32),
            pltpu.VMEM(leaf_shape, BF16),
            pltpu.VMEM((leaves, kernels, points, near * points), BF16),
            pltpu.VMEM((leaves, kernels, points, channels), BF16),
            pltpu.VMEM((leaves, near * points, channels), F32),
            pltpu.VMEM((received, points, channels), BF16),
            pltpu.VMEM((received, points, channels), BF16),
            pltpu.VMEM((leaves, near * points, channels), BF16),
            pltpu.VMEM((kernels, leaves * points, channels), BF16),
            pltpu.VMEM((kernels, leaves * points, half), BF16),
            pltpu.VMEM((kernels, half, channels), BF16),
            pltpu.VMEM((kernels, half // narrow, channels), BF16),
            pltpu.VMEM((wide - 1, kernels, band, channels), BF16),
            pltpu.VMEM((kernels, band, channels), BF16),
            pltpu.VMEM((wide - 1, kernels, tile, channels), BF16),
            pltpu.VMEM((padded, tile, channels), BF16),
            pltpu.VMEM((CHUNKS, nz - 1, CHUNK // nz, tile, channels), BF16),
            pltpu.VMEM((CHUNKS, CHUNK // nz, tile, channels), BF16),
            pltpu.VMEM((padded, tile, channels), BF16),
            pltpu.VMEM((kernels, band, channels), BF16),
            pltpu.SemaphoreType.DMA((8,)),
            pltpu.SemaphoreType.DMA((copies,)),
            pltpu.SemaphoreType.DMA((copies,)),
        ],
        compiler_params=pltpu.CompilerParams(
            collective_id=0, has_side_effects=True, vmem_limit_bytes=48 * 1024 * 1024
        ),
        name="convolution",
    )(
        *(
            pltpu.with_memory_space_constraint(operand, pltpu.HBM)
            for operand in (
                features[0], coords.transpose(1, 0, 2), kernel_points.T, weights.reshape(cube), support_slot[0],
                slot_mask[0], send_leaf[0, 0].T, cotangent[0],
            )
        )
    )
    output, grad, grad_weight = pl.pallas_call(
        write_kernel,
        out_shape=(
            jax.ShapeDtypeStruct(leaf_shape, BF16),
            jax.ShapeDtypeStruct(leaf_shape, BF16),
            jax.ShapeDtypeStruct(cube, F32),
        ),
        in_specs=[vmem, vmem, vmem],
        out_specs=(hbm, hbm, hbm),
        scratch_shapes=[pltpu.VMEM(cube, F32), pltpu.SemaphoreType.DMA((2 + kernels,))],
        compiler_params=pltpu.CompilerParams(vmem_limit_bytes=16 * 1024 * 1024),
        name="write",
    )(output, grad, mean)
    return (output[None], grad[None], grad_weight.reshape(kernels * channels, channels))


def solution(mesh):
    in_specs = (
        P("rep", "dom", None, None),
        P("rep", None, "dom"),
        P(),
        P(),
        P("rep", "dom", None),
        P("rep", "dom", None, None, None),
        P("rep", "dom", None, None),
        P("rep", "dom", None, None),
    )
    out_specs = (P("rep", "dom", None, None), P("rep", "dom", None, None), P())
    return jax.shard_map(shards, mesh=mesh, in_specs=in_specs, out_specs=out_specs, check_vma=False)
```

```python
import functools

import jax
import jax.numpy as jnp
from jax import lax
from jax.experimental import pallas as pl
from jax.experimental.pallas import tpu as pltpu
from jax.sharding import PartitionSpec as P

QUANT = 0.0625
EPSILON = 1e-06
CORES = 2
NY = 4
CHUNK = 8
CHUNKS = 2
MESH = pl.DeviceIdType.MESH
F32, BF16 = jnp.float32, jnp.bfloat16


def place():
    dom, rep = lax.axis_index("dom"), lax.axis_index("rep")
    return rep // CORES, lax.rem(dom, NY), dom // NY, lax.rem(rep, CORES)


def device(x, y, z, core):
    return (z * NY + y, x * CORES + core)


def greet(others):
    barrier = pltpu.get_barrier_semaphore()
    for other in others:
        pl.semaphore_signal(barrier, inc=1, device_id=other, device_id_type=MESH)


def all_here(count):
    pl.semaphore_wait(pltpu.get_barrier_semaphore(), count)


def steps_of(count):
    return sorted(range(1, count), key=lambda step: -min(step, count - step))


def around(position, count):
    return [lax.rem(position + step, count) for step in steps_of(count)]


def product(left, right, dims):
    return lax.dot_general(left, right, (dims, ((), ())), preferred_element_type=F32)


def batches(nx):
    return 5 + 2 * CHUNKS * (5 + nx + 1) + 2 * CHUNKS


def kernel(
    nx, nz, kernels, rounds,
    feats_in, coords_in, kernel_points_in, weights_in, slots_in, mask_in, sends_in, cot_in,
    output, grad, final,
    feats, coords, kernel_points, weights, slots, mask, sends, cot, pool_feats, pool_pos, own_pos, send_feats, send_pos, query, cot_pair, h, grad_summed, grad_support,
    send_grad, got_grad, support, summed, summed_pair, partial, partial_pair, got_first, part, got_second,
    slab, got_z, piece, gather_z, gather_second,
    local_sem, send_sem, recv_sem,
):
    leaves, points, channels = feats.shape
    near = slots.shape[1]
    bound = sends.shape[0]
    x, y, z, core = place()
    dom = z * NY + y
    sibling = device(x, y, z, 1 - core)
    axes = {
        "x": (x, nx, lambda o, c: device(o, y, z, c)),
        "y": (y, NY, lambda o, c: device(x, o, z, c)),
        "z": (z, nz, lambda o, c: device(x, y, o, c)),
    }
    low = NY.bit_length() - 1
    partners = []
    for bit in range(rounds):
        if bit < low:
            side = 1 << bit
            partners.append(device(x, y + side - 2 * side * lax.rem(y // side, 2), z, core))
        else:
            side = 1 << (bit - low)
            partners.append(device(x, y, z + side - 2 * side * lax.rem(z // side, 2), core))
    rings = {axis: [(to, o) for o in around(at, count)] for axis, (at, count, to) in axes.items()}
    plane = rings["x"] + rings["y"]

    @pl.when(core == 1)
    def _():
        greet([sibling] + [to(o, 1) for to, o in plane + rings["z"]] + [to(o, 0) for to, o in plane])

    @pl.when(core == 0)
    def _():
        greet([sibling] + partners + [to(o, 1) for to, o in plane])

    loads = {}
    for index, (name, src, dst) in enumerate((
        ("sends", sends_in, sends), ("coords", coords_in, coords), ("feats", feats_in, feats),
        ("cot", cot_in, cot), ("slots", slots_in, slots), ("points", kernel_points_in, kernel_points),
        ("weights", weights_in, weights), ("mask", mask_in, mask),
    )):
        loads[name] = pltpu.make_async_copy(src, dst, local_sem.at[index])
        loads[name].start()

    number = [0]

    def batch():
        number[0] += 1
        return number[0] - 1

    def describe(index, src, dst, other):
        return pltpu.make_async_remote_copy(
            src_ref=src, dst_ref=dst, send_sem=send_sem.at[index], recv_sem=recv_sem.at[index],
            device_id=other, device_id_type=MESH,
        )

    def push(index, src, dst, other):
        describe(index, src, dst, other).start()

    def arrived(index, like):
        pltpu.make_async_copy(like, like, recv_sem.at[index]).wait()

    def departed(index, like):
        pltpu.make_async_copy(like, like, send_sem.at[index]).wait()

    for name in ("sends", "coords", "feats"):
        loads[name].wait()
    positions = coords[...].reshape(3, leaves * points).astype(F32) * QUANT
    for leaf in range(leaves):
        own = positions[:, leaf * points : (leaf + 1) * points]
        both = jnp.concatenate([own, own], 1)
        own_pos[leaf] = jnp.concatenate([both, jnp.zeros((8 - 3, 2 * points), F32)], 0)
        pool_pos[leaf] = own_pos[leaf]
        pool_feats[leaf] = feats[leaf]
    for bit in range(rounds):
        for t in range(bound):
            chosen = sends[t, bit]
            send_feats[bit * bound + t] = feats[chosen]
            send_pos[bit * bound + t] = own_pos[chosen]

    @pl.when(core == 1)
    def _():
        all_here(1 + 2 * len(plane) + len(rings["z"]))

    @pl.when(core == 0)
    def _():
        all_here(1 + len(partners) + len(plane))

    batch_pos, batch_feats, batch_cot, batch_far, batch_near = (batch() for _ in range(5))
    for bit in reversed(range(rounds)):
        entry, there = pl.ds(bit * bound, bound), pl.ds(leaves + bit * bound, bound)
        push(batch_pos, send_pos.at[entry], pool_pos.at[there], partners[bit])
    for bit in reversed(range(rounds)):
        entry, there = pl.ds(bit * bound, bound), pl.ds(leaves + bit * bound, bound)
        push(batch_feats, send_feats.at[entry], pool_feats.at[there], partners[bit])
    received = pl.ds(leaves, rounds * bound)
    loads["cot"].wait()
    copy_cot = describe(batch_cot, cot, cot_pair, sibling)
    copy_cot.start()

    rows = lax.broadcasted_iota(jnp.int32, (points, 2 * points), 0)
    lanes = lax.broadcasted_iota(jnp.int32, (points, 2 * points), 1)
    for leaf in range(leaves):
        for c in range(3):
            line = jnp.where(rows == lanes, pool_pos[leaf, c : c + 1, :], 0.0)
            query[c, leaf] = jnp.broadcast_to(jnp.sum(line, 1, keepdims=True), (points, 2 * points))

    loads["weights"].wait()

    upstream = cot[...].reshape(leaves * points, channels)
    for k in range(kernels):
        block = product(upstream, weights[k], ((1,), (1,)))
        grad_summed[:, k] = block.astype(BF16).reshape(leaves, points, channels)

    for name in ("slots", "points", "mask"):
        loads[name].wait()
    arrived(batch_pos, pool_pos.at[received])

    def correlate(leaf, _):
        for pair in range(near // 2):
            first = pool_pos[slots[leaf, 2 * pair]]
            second = pool_pos[slots[leaf, 2 * pair + 1]]
            lane = lax.broadcasted_iota(jnp.int32, first.shape, 1)
            places = jnp.where(lane < points, first, second)
            apart = [places[c : c + 1, :] - query[c, leaf] for c in range(3)]
            shown = jnp.concatenate([mask[leaf, 2 * pair], mask[leaf, 2 * pair + 1]], 1).astype(F32)

            for k in range(kernels):
                squared = jnp.full(shown.shape, EPSILON, F32)
                for c in range(3):
                    difference = apart[c] - kernel_points[c, k]
                    squared = squared + difference * difference
                weight = jnp.maximum(1.0 - squared * lax.rsqrt(squared), 0.0) * shown
                h[leaf, k, :, pair * 2 * points : (pair + 1) * 2 * points] = weight.astype(BF16)
        return 0

    lax.fori_loop(0, leaves, correlate, 0)

    half = channels // CORES
    own_half = pl.ds(pl.multiple_of(core * half, half), half)
    pair_half = pl.ds(pl.multiple_of((1 - core) * half, half), half)
    chunks = [(k0, min(CHUNK, kernels - k0)) for k0 in range(0, kernels, CHUNK)]
    groups = []
    for k0, nk in chunks:
        cut = (nk + 1) // 2
        groups.append([(k0, cut, "x", "y"), (k0 + cut, nk - cut, "y", "x")])
    pairs = sum(groups, [])

    def band(axis, at, start=0):
        block = half // axes[axis][1]
        return pl.ds(pl.multiple_of(start + at * block, block), block)

    def tile(axis, at):
        block = part.shape[1] // axes[axis][1]
        return pl.ds(pl.multiple_of(at * block, block), block)

    halves, firsts, owns, fronts, back_own, lasts = ({} for _ in range(6))
    batch_first, batch_second, batch_back, batch_front, batch_last = ({} for _ in range(5))
    for g0, ng, first, _ in pairs:
        there = pl.ds(g0, ng)
        at, count, to = axes[first]
        block = half // count
        halves[g0] = describe(batch(), summed.at[there, :, pair_half], summed_pair.at[there], sibling)
        for table in (batch_first, batch_second, batch_back, batch_last):
            table[g0] = batch()
        for step, o in zip(steps_of(count), around(at, count)):
            batch_front[g0, step] = batch()
            for side in range(CORES):
                rows = pl.ds(side * block, block)
                firsts[g0, step, side] = describe(
                    batch_first[g0], partial.at[there, band(first, o), :], got_first.at[step - 1, there, rows, :],
                    to(o, 1),
                )
                fronts[g0, step, side] = describe(
                    batch_front[g0, step], gather_second.at[there, rows, :],
                    final.at[there, band(first, at, side * half), :], to(o, side),
                )
        owns[g0] = describe(batch(), partial.at[there, band(first, at), :], partial_pair.at[there], sibling)
        back_own[g0] = describe(
            batch(), gather_second.at[there, pl.ds(0, block), :], final.at[there, band(first, at), :], sibling
        )
        for step in range(count):
            here = final.at[there, band(first, lax.rem(at + count - step, count), core * half), :]
            lasts[g0, step] = describe(batch_last[g0], here, here, sibling)
    batch_z, batch_back_z = ([batch() for _ in chunks] for _ in range(2))

    def bands(g0, ng, first, count):
        return final.at[pl.ds(g0, ng), pl.ds(0, count * (half // axes[first][1])), :]

    arrived(batch_feats, pool_feats.at[received])
    for leaf in range(leaves):
        for n in range(near):
            support[leaf, n * points : (n + 1) * points, :] = pool_feats[slots[leaf, n]]
    for g0, ng, _, _ in pairs:
        for leaf in range(leaves):
            left = h[leaf, g0 : g0 + ng].reshape(ng * points, near * points)
            block = product(left, support[leaf], ((1,), (0,))).astype(BF16)
            summed[g0 : g0 + ng, leaf * points : (leaf + 1) * points, :] = block.reshape(ng, points, channels)
        halves[g0].start()

    copy_cot.wait_recv()
    upstream_pair = cot_pair[...].reshape(leaves * points, channels)
    for g0, ng, first, _ in pairs:
        halves[g0].wait_recv()
        for k in range(g0, g0 + ng):
            block = product(summed[k, :, own_half].T, upstream, ((1,), (0,)))
            block += product(summed_pair[k].T, upstream_pair, ((1,), (0,)))
            partial[k] = block.astype(BF16)
        for side in range(CORES):

            @pl.when(core == side)
            def _():
                for step in steps_of(axes[first][1]):
                    firsts[g0, step, side].start()
                if side == 0:
                    owns[g0].start()

    def gathered(entry, total):
        for leaf in range(leaves):
            for n in range(1, near):
                named = jnp.where(slots[leaf, n] == entry, 1.0, 0.0)
                total = total + named * grad_support[leaf, n * points : (n + 1) * points, :]
        return total

    def away(entry, _):
        send_grad[entry] = gathered(entry + leaves, jnp.zeros((points, channels), F32)).astype(BF16)
        return 0

    def feature_gradients():
        for leaf in range(leaves):
            left = h[leaf].reshape(kernels * points, near * points)
            right = grad_summed[leaf].reshape(kernels * points, channels)
            grad_support[leaf] = product(left, right, ((0,), (0,)))
        lax.fori_loop(0, rounds * bound, away, 0)

    def hand_back(index, bits):
        for bit in reversed(bits):
            entry = pl.ds(bit * bound, bound)
            push(index, send_grad.at[entry], got_grad.at[entry], partners[bit])

    far, near_by = pl.ds(low * bound, (rounds - low) * bound), pl.ds(0, low * bound)

    def handed_back():
        arrived(batch_far, got_grad.at[far])
        arrived(batch_near, got_grad.at[near_by])
        lax.fori_loop(0, leaves, owned, 0)
        departed(batch_far, send_grad.at[far])
        departed(batch_near, send_grad.at[near_by])
        departed(batch_pos, send_pos)
        departed(batch_feats, send_feats)
        copy_cot.wait_send()
        for copy in halves.values():
            copy.wait_send()

    def first_left():
        for g0, ng, first, _ in pairs:
            departed(batch_first[g0], bands(g0, ng, first, axes[first][1] - 1))

    def outputs():
        total = product(summed[0], weights[0], ((1,), (0,)))
        for k in range(1, kernels):
            total = total + product(summed[k], weights[k], ((1,), (0,)))
        output[...] = total.astype(BF16).reshape(output.shape)

    def owned(leaf, _):
        total = gathered(leaf, grad_support[leaf, 0:points, :])
        for bit in range(rounds):
            for t in range(bound):
                named = jnp.where(sends[t, bit] == leaf, 1.0, 0.0)
                total = total + named * got_grad[bit * bound + t].astype(F32)
        grad[leaf] = total.astype(BF16)
        return 0

    def exchange(side):
        for g0, ng, first, _ in pairs:
            for step in steps_of(axes[first][1])[::-1]:
                fronts[g0, step, side].wait_recv()
                lasts[g0, step].start()
            if side == 0:
                back_own[g0].wait_recv()
        for g0, ng, first, _ in pairs:
            count = axes[first][1]
            arrived(batch_last[g0], bands(g0, ng, first, count - side))
            departed(batch_last[g0], bands(g0, ng, first, count - 1 + side))

    @pl.when(core == 0)
    def _():
        feature_gradients()
        hand_back(batch_far, range(low, rounds))
        outputs()
        first_left()
        hand_back(batch_near, range(low))
        handed_back()
        for copy in owns.values():
            copy.wait_send()
        exchange(0)

    @pl.when(core == 1)
    def _():
        feature_gradients()
        hand_back(batch_far, range(low, rounds))
        outputs()

        for g0, ng, first, second in pairs:
            at, count, _ = axes[first]
            block = half // count
            there = pl.ds(g0, ng)
            owns[g0].wait_recv()
            arrived(batch_first[g0], got_first.at[:, there])
            for k in range(g0, g0 + ng):
                for side, own in ((0, partial_pair[k]), (1, partial[k, band(first, at), :])):
                    rows = slice(side * block, (side + 1) * block)
                    total = own.astype(F32)
                    for step in range(count - 1):
                        total = total + got_first[step, k, rows, :].astype(F32)
                    part[k, rows, :] = total.astype(BF16)
            at, count, to = axes[second]
            for step, o in enumerate(around(at, count)):
                push(batch_second[g0], part.at[there, tile(second, o), :], got_second.at[step, there], to(o, 1))
        hand_back(batch_near, range(low))

        per_z = CHUNK // nz
        for index, (k0, nk) in enumerate(chunks):
            base = index * CHUNK - k0
            for k in range(k0 + nk, k0 + CHUNK):
                slab[base + k] = jnp.zeros(slab.shape[1:], BF16)
            for g0, ng, _, second in groups[index]:
                arrived(batch_second[g0], got_second.at[:, pl.ds(g0, ng)])
                at, count, _ = axes[second]
                for k in range(g0, g0 + ng):
                    total = part[k, tile(second, at), :].astype(F32)
                    for step in range(count - 1):
                        total = total + got_second[step, k].astype(F32)
                    slab[base + k] = total.astype(BF16)
            at, count, to = axes["z"]
            for step, o in enumerate(around(at, count)):
                push(batch_z[index], slab.at[pl.ds(index * CHUNK + o * per_z, per_z)], got_z.at[index, step], to(o, 1))
        devices = nx * NY * nz * CORES
        for index in range(CHUNKS):
            arrived(batch_z[index], got_z.at[index])
            at, count, to = axes["z"]
            own = pl.ds(index * CHUNK + z * per_z, per_z)
            total = slab[own].astype(F32)
            for step in range(count - 1):
                total = total + got_z[index, step].astype(F32)
            piece[index] = (total / devices).astype(BF16)
            for o in around(at, count):
                push(batch_back_z[index], piece.at[index], gather_z.at[own], to(o, 1))
            gather_z[own] = piece[index]

        handed_back()
        first_left()

        for index, (k0, nk) in enumerate(chunks):
            arrived(batch_back_z[index], got_z.at[index])
            for g0, ng, _, second in groups[index]:
                at, count, to = axes[second]
                there, here = pl.ds(g0, ng), pl.ds(index * CHUNK + g0 - k0, ng)
                own = tile(second, at)
                for o in around(at, count):
                    push(batch_back[g0], gather_z.at[here], gather_second.at[there, own, :], to(o, 1))
                gather_second[there, own, :] = gather_z[here]
        for g0, ng, first, _ in pairs:
            there = pl.ds(g0, ng)
            arrived(batch_back[g0], got_second.at[:, there])
            at, count, _ = axes[first]
            block = half // count
            for step in steps_of(count):
                for side in range(CORES):
                    fronts[g0, step, side].start()
            back_own[g0].start()
            for side in range(CORES):
                rows = slice(side * block, (side + 1) * block)
                final[there, band(first, at, side * half), :] = gather_second[there, rows, :]
            lasts[g0, 0].start()
        for index in range(CHUNKS):
            departed(batch_z[index], got_z.at[index])
            departed(batch_back_z[index], got_z.at[index])
        for g0, ng, _, _ in pairs:
            departed(batch_second[g0], got_second.at[:, pl.ds(g0, ng)])
            departed(batch_back[g0], got_second.at[:, pl.ds(g0, ng)])
        exchange(1)
        for g0, ng, first, _ in pairs:
            back_own[g0].wait_send()
            for step in steps_of(axes[first][1]):
                departed(batch_front[g0, step], gather_second.at[pl.ds(g0, ng)])


def write_kernel(output, grad, mean, output_out, grad_out, mean_out, wide, sem):
    copies = []
    for index, (src, dst) in enumerate(((output, output_out), (grad, grad_out))):
        copies.append(pltpu.make_async_copy(src, dst, sem.at[index]))
        copies[-1].start()
    for k in range(mean.shape[0]):
        wide[k] = mean[k].astype(F32)
        copies.append(pltpu.make_async_copy(wide.at[k], mean_out.at[k], sem.at[2 + k]))
        copies[-1].start()
    for copy in copies:
        copy.wait()


def shards(features, coords, kernel_points, weights, support_slot, slot_mask, send_leaf, cotangent):
    leaves, points, channels = features.shape[1:]
    kernels = kernel_points.shape[0]
    near = support_slot.shape[2]
    nx, nz = lax.axis_size("rep") // CORES, lax.axis_size("dom") // NY
    rounds = lax.axis_size("dom").bit_length() - 1
    bound = send_leaf.shape[3]
    received = rounds * bound
    padded = CHUNKS * CHUNK
    half = channels // CORES
    wide, narrow = max(nx, NY), min(nx, NY)
    band, tile = channels // narrow, channels // (nx * NY)
    copies = batches(max(nx, NY))
    vmem, hbm = (pl.BlockSpec(memory_space=space) for space in (pltpu.VMEM, pltpu.HBM))
    cube = (kernels, channels, channels)
    leaf_shape = (leaves, points, channels)
    output, grad, mean = pl.pallas_call(
        functools.partial(kernel, nx, nz, kernels, rounds),
        out_shape=(
            jax.ShapeDtypeStruct(leaf_shape, BF16),
            jax.ShapeDtypeStruct(leaf_shape, BF16),
            jax.ShapeDtypeStruct(cube, BF16),
        ),
        in_specs=[hbm] * 8,
        out_specs=(vmem, vmem, vmem),
        scratch_shapes=[
            pltpu.VMEM(leaf_shape, BF16),
            pltpu.VMEM((3, 1, leaves * points), jnp.int32),
            pltpu.SMEM((3, kernels), F32),
            pltpu.VMEM(cube, BF16),
            pltpu.SMEM((leaves, near), jnp.int32),
            pltpu.VMEM(slot_mask.shape[1:], jnp.int32),
            pltpu.SMEM((bound, rounds), jnp.int32),
            pltpu.VMEM(leaf_shape, BF16),
            pltpu.VMEM((leaves + received, points, channels), BF16),
            pltpu.VMEM((leaves + received, 8, 2 * points), F32),
            pltpu.VMEM((leaves, 8, 2 * points), F32),
            pltpu.VMEM((received, points, channels), BF16),
            pltpu.VMEM((received, 8, 2 * points), F32),
            pltpu.VMEM((3, leaves, points, 2 * points), F32),
            pltpu.VMEM(leaf_shape, BF16),
            pltpu.VMEM((leaves, kernels, points, near * points), BF16),
            pltpu.VMEM((leaves, kernels, points, channels), BF16),
            pltpu.VMEM((leaves, near * points, channels), F32),
            pltpu.VMEM((received, points, channels), BF16),
            pltpu.VMEM((received, points, channels), BF16),
            pltpu.VMEM((leaves, near * points, channels), BF16),
            pltpu.VMEM((kernels, leaves * points, channels), BF16),
            pltpu.VMEM((kernels, leaves * points, half), BF16),
            pltpu.VMEM((kernels, half, channels), BF16),
            pltpu.VMEM((kernels, half // narrow, channels), BF16),
            pltpu.VMEM((wide - 1, kernels, band, channels), BF16),
            pltpu.VMEM((kernels, band, channels), BF16),
            pltpu.VMEM((wide - 1, kernels, tile, channels), BF16),
            pltpu.VMEM((padded, tile, channels), BF16),
            pltpu.VMEM((CHUNKS, nz - 1, CHUNK // nz, tile, channels), BF16),
            pltpu.VMEM((CHUNKS, CHUNK // nz, tile, channels), BF16),
            pltpu.VMEM((padded, tile, channels), BF16),
            pltpu.VMEM((kernels, band, channels), BF16),
            pltpu.SemaphoreType.DMA((8,)),
            pltpu.SemaphoreType.DMA((copies,)),
            pltpu.SemaphoreType.DMA((copies,)),
        ],
        compiler_params=pltpu.CompilerParams(
            collective_id=0, has_side_effects=True, vmem_limit_bytes=48 * 1024 * 1024
        ),
        name="convolution",
    )(
        *(
            pltpu.with_memory_space_constraint(operand, pltpu.HBM)
            for operand in (
                features[0], coords.transpose(1, 0, 2), kernel_points.T, weights.reshape(cube), support_slot[0],
                slot_mask[0], send_leaf[0, 0].T, cotangent[0],
            )
        )
    )
    output, grad, grad_weight = pl.pallas_call(
        write_kernel,
        out_shape=(
            jax.ShapeDtypeStruct(leaf_shape, BF16),
            jax.ShapeDtypeStruct(leaf_shape, BF16),
            jax.ShapeDtypeStruct(cube, F32),
        ),
        in_specs=[vmem, vmem, vmem],
        out_specs=(hbm, hbm, hbm),
        scratch_shapes=[pltpu.VMEM(cube, F32), pltpu.SemaphoreType.DMA((2 + kernels,))],
        compiler_params=pltpu.CompilerParams(vmem_limit_bytes=16 * 1024 * 1024),
        name="write",
    )(output, grad, mean)
    return (output[None], grad[None], grad_weight.reshape(kernels * channels, channels))


def solution(mesh):
    in_specs = (
        P("rep", "dom", None, None),
        P("rep", None, "dom"),
        P(),
        P(),
        P("rep", "dom", None),
        P("rep", "dom", None, None, None),
        P("rep", "dom", None, None),
        P("rep", "dom", None, None),
    )
    out_specs = (P("rep", "dom", None, None), P("rep", "dom", None, None), P())
    return jax.shard_map(shards, mesh=mesh, in_specs=in_specs, out_specs=out_specs, check_vma=False)
```

```python
import functools

import jax
import jax.numpy as jnp
from jax import lax
from jax.experimental import pallas as pl
from jax.experimental.pallas import tpu as pltpu
from jax.sharding import PartitionSpec as P

QUANT = 0.0625
EPSILON = 1e-06
CORES = 2
NY = 4
CHUNK = 8
CHUNKS = 2
MESH = pl.DeviceIdType.MESH
F32, BF16 = jnp.float32, jnp.bfloat16


def place():
    dom, rep = lax.axis_index("dom"), lax.axis_index("rep")
    return rep // CORES, lax.rem(dom, NY), dom // NY, lax.rem(rep, CORES)


def device(x, y, z, core):
    return (z * NY + y, x * CORES + core)


def greet(others):
    barrier = pltpu.get_barrier_semaphore()
    for other in others:
        pl.semaphore_signal(barrier, inc=1, device_id=other, device_id_type=MESH)


def all_here(count):
    pl.semaphore_wait(pltpu.get_barrier_semaphore(), count)


def steps_of(count):
    return sorted(range(1, count), key=lambda step: -min(step, count - step))


def around(position, count):
    return [lax.rem(position + step, count) for step in steps_of(count)]


def product(left, right, dims):
    return lax.dot_general(left, right, (dims, ((), ())), preferred_element_type=F32)


def batches(nx):
    return 5 + 2 * CHUNKS * (5 + nx + 1) + 2 * CHUNKS


def kernel(
    nx, nz, kernels, rounds,
    feats_in, coords_in, kernel_points_in, weights_in, slots_in, mask_in, sends_in, cot_in,
    output, grad, final,
    feats, coords, kernel_points, weights, slots, mask, sends, cot, pool_feats, pool_pos, own_pos, send_feats, send_pos, query, cot_pair, h, grad_summed, grad_support,
    send_grad, got_grad, support, summed, summed_pair, partial, partial_pair, got_first, part, got_second,
    slab, got_z, piece, gather_z, gather_second,
    local_sem, send_sem, recv_sem,
):
    leaves, points, channels = feats.shape
    near = slots.shape[1]
    bound = sends.shape[0]
    x, y, z, core = place()
    dom = z * NY + y
    sibling = device(x, y, z, 1 - core)
    axes = {
        "x": (x, nx, lambda o, c: device(o, y, z, c)),
        "y": (y, NY, lambda o, c: device(x, o, z, c)),
        "z": (z, nz, lambda o, c: device(x, y, o, c)),
    }
    low = NY.bit_length() - 1
    partners = []
    for bit in range(rounds):
        if bit < low:
            side = 1 << bit
            partners.append(device(x, y + side - 2 * side * lax.rem(y // side, 2), z, core))
        else:
            side = 1 << (bit - low)
            partners.append(device(x, y, z + side - 2 * side * lax.rem(z // side, 2), core))
    rings = {axis: [(to, o) for o in around(at, count)] for axis, (at, count, to) in axes.items()}
    plane = rings["x"] + rings["y"]

    @pl.when(core == 1)
    def _():
        greet([to(o, 1) for to, o in rings["z"] + plane] + [to(o, 0) for to, o in plane] + [sibling])

    @pl.when(core == 0)
    def _():
        greet(partners[::-1] + [to(o, 1) for to, o in plane] + [sibling])

    loads = {}
    for index, (name, src, dst) in enumerate((
        ("sends", sends_in, sends), ("coords", coords_in, coords), ("feats", feats_in, feats),
        ("cot", cot_in, cot), ("slots", slots_in, slots), ("points", kernel_points_in, kernel_points),
        ("weights", weights_in, weights), ("mask", mask_in, mask),
    )):
        loads[name] = pltpu.make_async_copy(src, dst, local_sem.at[index])
    early = ("sends", "coords", "feats")
    for name in early:
        loads[name].start()

    number = [0]

    def batch():
        number[0] += 1
        return number[0] - 1

    def describe(index, src, dst, other):
        return pltpu.make_async_remote_copy(
            src_ref=src, dst_ref=dst, send_sem=send_sem.at[index], recv_sem=recv_sem.at[index],
            device_id=other, device_id_type=MESH,
        )

    def push(index, src, dst, other):
        describe(index, src, dst, other).start()

    def arrived(index, like):
        pltpu.make_async_copy(like, like, recv_sem.at[index]).wait()

    def departed(index, like):
        pltpu.make_async_copy(like, like, send_sem.at[index]).wait()

    for name in early:
        loads[name].wait()
    for name in loads:
        if name not in early:
            loads[name].start()
    positions = coords[...].reshape(3, leaves * points).astype(F32) * QUANT
    for leaf in range(leaves):
        own = positions[:, leaf * points : (leaf + 1) * points]
        both = jnp.concatenate([own, own], 1)
        own_pos[leaf] = jnp.concatenate([both, jnp.zeros((8 - 3, 2 * points), F32)], 0)
        pool_pos[leaf] = own_pos[leaf]
        pool_feats[leaf] = feats[leaf]
    for bit in range(rounds):
        for t in range(bound):
            chosen = sends[t, bit]
            send_feats[bit * bound + t] = feats[chosen]
            send_pos[bit * bound + t] = own_pos[chosen]

    @pl.when(core == 1)
    def _():
        all_here(1 + 2 * len(plane) + len(rings["z"]))

    @pl.when(core == 0)
    def _():
        all_here(1 + len(partners) + len(plane))

    batch_pos, batch_feats, batch_cot, batch_far, batch_near = (batch() for _ in range(5))
    for bit in reversed(range(rounds)):
        entry, there = pl.ds(bit * bound, bound), pl.ds(leaves + bit * bound, bound)
        push(batch_pos, send_pos.at[entry], pool_pos.at[there], partners[bit])
    for bit in reversed(range(rounds)):
        entry, there = pl.ds(bit * bound, bound), pl.ds(leaves + bit * bound, bound)
        push(batch_feats, send_feats.at[entry], pool_feats.at[there], partners[bit])
    received = pl.ds(leaves, rounds * bound)
    loads["cot"].wait()
    copy_cot = describe(batch_cot, cot, cot_pair, sibling)
    copy_cot.start()

    rows = lax.broadcasted_iota(jnp.int32, (points, 2 * points), 0)
    lanes = lax.broadcasted_iota(jnp.int32, (points, 2 * points), 1)
    for leaf in range(leaves):
        for c in range(3):
            line = jnp.where(rows == lanes, pool_pos[leaf, c : c + 1, :], 0.0)
            query[c, leaf] = jnp.broadcast_to(jnp.sum(line, 1, keepdims=True), (points, 2 * points))

    loads["weights"].wait()

    upstream = cot[...].reshape(leaves * points, channels)
    for k in range(kernels):
        block = product(upstream, weights[k], ((1,), (1,)))
        grad_summed[:, k] = block.astype(BF16).reshape(leaves, points, channels)

    for name in ("slots", "points", "mask"):
        loads[name].wait()
    arrived(batch_pos, pool_pos.at[received])

    def correlate(leaf, _):
        for pair in range(near // 2):
            first = pool_pos[slots[leaf, 2 * pair]]
            second = pool_pos[slots[leaf, 2 * pair + 1]]
            lane = lax.broadcasted_iota(jnp.int32, first.shape, 1)
            places = jnp.where(lane < points, first, second)
            apart = [places[c : c + 1, :] - query[c, leaf] for c in range(3)]
            shown = jnp.concatenate([mask[leaf, 2 * pair], mask[leaf, 2 * pair + 1]], 1).astype(F32)

            for k in range(kernels):
                squared = jnp.full(shown.shape, EPSILON, F32)
                for c in range(3):
                    difference = apart[c] - kernel_points[c, k]
                    squared = squared + difference * difference
                weight = jnp.maximum(1.0 - squared * lax.rsqrt(squared), 0.0) * shown
                h[leaf, k, :, pair * 2 * points : (pair + 1) * 2 * points] = weight.astype(BF16)
        return 0

    lax.fori_loop(0, leaves, correlate, 0)

    half = channels // CORES
    own_half = pl.ds(pl.multiple_of(core * half, half), half)
    pair_half = pl.ds(pl.multiple_of((1 - core) * half, half), half)
    chunks = [(k0, min(CHUNK, kernels - k0)) for k0 in range(0, kernels, CHUNK)]
    groups = []
    for k0, nk in chunks:
        cut = (nk + 1) // 2
        if k0 == 0:
            groups.append([(k0, cut, "x", "y"), (k0 + cut, nk - cut, "y", "x")])
        else:
            groups.append([(k0, nk - cut, "y", "x"), (k0 + nk - cut, cut, "x", "y")])
    pairs = sum(groups, [])

    def band(axis, at, start=0):
        block = half // axes[axis][1]
        return pl.ds(pl.multiple_of(start + at * block, block), block)

    def tile(axis, at):
        block = part.shape[1] // axes[axis][1]
        return pl.ds(pl.multiple_of(at * block, block), block)

    halves, firsts, owns, fronts, back_own, lasts = ({} for _ in range(6))
    batch_first, batch_second, batch_back, batch_front, batch_last = ({} for _ in range(5))
    for g0, ng, first, _ in pairs:
        there = pl.ds(g0, ng)
        at, count, to = axes[first]
        block = half // count
        halves[g0] = describe(batch(), summed.at[there, :, pair_half], summed_pair.at[there], sibling)
        for table in (batch_first, batch_second, batch_back, batch_last):
            table[g0] = batch()
        for step, o in zip(steps_of(count), around(at, count)):
            batch_front[g0, step] = batch()
            for side in range(CORES):
                rows = pl.ds(side * block, block)
                firsts[g0, step, side] = describe(
                    batch_first[g0], partial.at[there, band(first, o), :], got_first.at[step - 1, there, rows, :],
                    to(o, 1),
                )
                fronts[g0, step, side] = describe(
                    batch_front[g0, step], gather_second.at[there, rows, :],
                    final.at[there, band(first, at, side * half), :], to(o, side),
                )
        owns[g0] = describe(batch(), partial.at[there, band(first, at), :], partial_pair.at[there], sibling)
        back_own[g0] = describe(
            batch(), gather_second.at[there, pl.ds(0, block), :], final.at[there, band(first, at), :], sibling
        )
        for step in range(count):
            here = final.at[there, band(first, lax.rem(at + count - step, count), core * half), :]
            lasts[g0, step] = describe(batch_last[g0], here, here, sibling)
    batch_z, batch_back_z = ([batch() for _ in chunks] for _ in range(2))

    def bands(g0, ng, first, count):
        return final.at[pl.ds(g0, ng), pl.ds(0, count * (half // axes[first][1])), :]

    arrived(batch_feats, pool_feats.at[received])
    for leaf in range(leaves):
        for n in range(near):
            support[leaf, n * points : (n + 1) * points, :] = pool_feats[slots[leaf, n]]
    for g0, ng, _, _ in pairs:
        for leaf in range(leaves):
            left = h[leaf, g0 : g0 + ng].reshape(ng * points, near * points)
            block = product(left, support[leaf], ((1,), (0,))).astype(BF16)
            summed[g0 : g0 + ng, leaf * points : (leaf + 1) * points, :] = block.reshape(ng, points, channels)
        halves[g0].start()

    copy_cot.wait_recv()
    upstream_pair = cot_pair[...].reshape(leaves * points, channels)
    for g0, ng, first, _ in pairs:
        halves[g0].wait_recv()
        for k in range(g0, g0 + ng):
            block = product(summed[k, :, own_half].T, upstream, ((1,), (0,)))
            block += product(summed_pair[k].T, upstream_pair, ((1,), (0,)))
            partial[k] = block.astype(BF16)
        for side in range(CORES):

            @pl.when(core == side)
            def _():
                for step in steps_of(axes[first][1]):
                    firsts[g0, step, side].start()
                if side == 0:
                    owns[g0].start()

    def gathered(entry, total):
        for leaf in range(leaves):
            for n in range(1, near):
                named = jnp.where(slots[leaf, n] == entry, 1.0, 0.0)
                total = total + named * grad_support[leaf, n * points : (n + 1) * points, :]
        return total

    def away(entry, _):
        send_grad[entry] = gathered(entry + leaves, jnp.zeros((points, channels), F32)).astype(BF16)
        return 0

    def feature_gradients():
        for leaf in range(leaves):
            left = h[leaf].reshape(kernels * points, near * points)
            right = grad_summed[leaf].reshape(kernels * points, channels)
            grad_support[leaf] = product(left, right, ((0,), (0,)))
        lax.fori_loop(0, rounds * bound, away, 0)

    def hand_back(index, bits):
        for bit in reversed(bits):
            entry = pl.ds(bit * bound, bound)
            push(index, send_grad.at[entry], got_grad.at[entry], partners[bit])

    far, near_by = pl.ds(low * bound, (rounds - low) * bound), pl.ds(0, low * bound)

    def handed_back():
        arrived(batch_far, got_grad.at[far])
        arrived(batch_near, got_grad.at[near_by])
        lax.fori_loop(0, leaves, owned, 0)
        departed(batch_far, send_grad.at[far])
        departed(batch_near, send_grad.at[near_by])
        departed(batch_pos, send_pos)
        departed(batch_feats, send_feats)
        copy_cot.wait_send()
        for copy in halves.values():
            copy.wait_send()

    def first_left():
        for g0, ng, first, _ in pairs:
            departed(batch_first[g0], bands(g0, ng, first, axes[first][1] - 1))

    def outputs():
        total = product(summed[0], weights[0], ((1,), (0,)))
        for k in range(1, kernels):
            total = total + product(summed[k], weights[k], ((1,), (0,)))
        output[...] = total.astype(BF16).reshape(output.shape)

    def owned(leaf, _):
        total = gathered(leaf, grad_support[leaf, 0:points, :])
        for bit in range(rounds):
            for t in range(bound):
                named = jnp.where(sends[t, bit] == leaf, 1.0, 0.0)
                total = total + named * got_grad[bit * bound + t].astype(F32)
        grad[leaf] = total.astype(BF16)
        return 0

    def exchange(side):
        for g0, ng, first, _ in pairs:
            for step in steps_of(axes[first][1])[::-1]:
                fronts[g0, step, side].wait_recv()
                lasts[g0, step].start()
            if side == 0:
                back_own[g0].wait_recv()
        for g0, ng, first, _ in pairs:
            count = axes[first][1]
            if side == 1:
                back_own[g0].wait_send()
                for step in steps_of(count):
                    departed(batch_front[g0, step], gather_second.at[pl.ds(g0, ng)])
            departed(batch_last[g0], bands(g0, ng, first, count - 1 + side))
        for g0, ng, first, _ in pairs:
            arrived(batch_last[g0], bands(g0, ng, first, axes[first][1] - side))

    feature_gradients()
    hand_back(batch_far, range(low, rounds))
    outputs()

    @pl.when(core == 0)
    def _():
        first_left()
        hand_back(batch_near, range(low))
        handed_back()
        for copy in owns.values():
            copy.wait_send()
        exchange(0)

    @pl.when(core == 1)
    def _():
        for g0, ng, first, second in pairs:
            at, count, _ = axes[first]
            block = half // count
            there = pl.ds(g0, ng)
            owns[g0].wait_recv()
            arrived(batch_first[g0], got_first.at[:, there])
            for k in range(g0, g0 + ng):
                for side, own in ((0, partial_pair[k]), (1, partial[k, band(first, at), :])):
                    rows = slice(side * block, (side + 1) * block)
                    total = own.astype(F32)
                    for step in range(count - 1):
                        total = total + got_first[step, k, rows, :].astype(F32)
                    part[k, rows, :] = total.astype(BF16)
            at, count, to = axes[second]
            for step, o in enumerate(around(at, count)):
                push(batch_second[g0], part.at[there, tile(second, o), :], got_second.at[step, there], to(o, 1))
        hand_back(batch_near, range(low))

        per_z = CHUNK // nz
        for index, (k0, nk) in enumerate(chunks):
            base = index * CHUNK - k0
            for k in range(k0 + nk, k0 + CHUNK):
                slab[base + k] = jnp.zeros(slab.shape[1:], BF16)
            for g0, ng, _, second in groups[index]:
                arrived(batch_second[g0], got_second.at[:, pl.ds(g0, ng)])
                at, count, _ = axes[second]
                for k in range(g0, g0 + ng):
                    total = part[k, tile(second, at), :].astype(F32)
                    for step in range(count - 1):
                        total = total + got_second[step, k].astype(F32)
                    slab[base + k] = total.astype(BF16)
            at, count, to = axes["z"]
            for step, o in enumerate(around(at, count)):
                push(batch_z[index], slab.at[pl.ds(index * CHUNK + o * per_z, per_z)], got_z.at[index, step], to(o, 1))
        devices = nx * NY * nz * CORES
        for index in range(CHUNKS):
            arrived(batch_z[index], got_z.at[index])
            at, count, to = axes["z"]
            own = pl.ds(index * CHUNK + z * per_z, per_z)
            total = slab[own].astype(F32)
            for step in range(count - 1):
                total = total + got_z[index, step].astype(F32)
            piece[index] = (total / devices).astype(BF16)
            for o in around(at, count):
                push(batch_back_z[index], piece.at[index], gather_z.at[own], to(o, 1))
            gather_z[own] = piece[index]

        handed_back()
        first_left()

        for index, (k0, nk) in enumerate(chunks):
            arrived(batch_back_z[index], got_z.at[index])
            for g0, ng, _, second in groups[index]:
                at, count, to = axes[second]
                there, here = pl.ds(g0, ng), pl.ds(index * CHUNK + g0 - k0, ng)
                own = tile(second, at)
                for o in around(at, count):
                    push(batch_back[g0], gather_z.at[here], gather_second.at[there, own, :], to(o, 1))
                gather_second[there, own, :] = gather_z[here]
        for g0, ng, first, _ in pairs:
            there = pl.ds(g0, ng)
            arrived(batch_back[g0], got_second.at[:, there])
            at, count, _ = axes[first]
            block = half // count
            for step in steps_of(count):
                for side in range(CORES):
                    fronts[g0, step, side].start()
            back_own[g0].start()
            for side in range(CORES):
                rows = slice(side * block, (side + 1) * block)
                final[there, band(first, at, side * half), :] = gather_second[there, rows, :]
        for g0, _, _, _ in pairs:
            lasts[g0, 0].start()
        for index in range(CHUNKS):
            departed(batch_z[index], got_z.at[index])
            departed(batch_back_z[index], got_z.at[index])
        for g0, ng, _, _ in pairs:
            departed(batch_second[g0], got_second.at[:, pl.ds(g0, ng)])
            departed(batch_back[g0], got_second.at[:, pl.ds(g0, ng)])
        exchange(1)


def write_kernel(output, grad, mean, output_out, grad_out, mean_out, wide, sem):
    copies = []
    for index, (src, dst) in enumerate(((output, output_out), (grad, grad_out))):
        copies.append(pltpu.make_async_copy(src, dst, sem.at[index]))
        copies[-1].start()
    for k in range(mean.shape[0]):
        wide[k] = mean[k].astype(F32)
        copies.append(pltpu.make_async_copy(wide.at[k], mean_out.at[k], sem.at[2 + k]))
        copies[-1].start()
    for copy in copies:
        copy.wait()


def shards(features, coords, kernel_points, weights, support_slot, slot_mask, send_leaf, cotangent):
    leaves, points, channels = features.shape[1:]
    kernels = kernel_points.shape[0]
    near = support_slot.shape[2]
    nx, nz = lax.axis_size("rep") // CORES, lax.axis_size("dom") // NY
    rounds = lax.axis_size("dom").bit_length() - 1
    bound = send_leaf.shape[3]
    received = rounds * bound
    padded = CHUNKS * CHUNK
    half = channels // CORES
    wide, narrow = max(nx, NY), min(nx, NY)
    band, tile = channels // narrow, channels // (nx * NY)
    copies = batches(max(nx, NY))
    vmem, hbm = (pl.BlockSpec(memory_space=space) for space in (pltpu.VMEM, pltpu.HBM))
    cube = (kernels, channels, channels)
    leaf_shape = (leaves, points, channels)
    output, grad, mean = pl.pallas_call(
        functools.partial(kernel, nx, nz, kernels, rounds),
        out_shape=(
            jax.ShapeDtypeStruct(leaf_shape, BF16),
            jax.ShapeDtypeStruct(leaf_shape, BF16),
            jax.ShapeDtypeStruct(cube, BF16),
        ),
        in_specs=[hbm] * 8,
        out_specs=(vmem, vmem, vmem),
        scratch_shapes=[
            pltpu.VMEM(leaf_shape, BF16),
            pltpu.VMEM((3, 1, leaves * points), jnp.int32),
            pltpu.SMEM((3, kernels), F32),
            pltpu.VMEM(cube, BF16),
            pltpu.SMEM((leaves, near), jnp.int32),
            pltpu.VMEM(slot_mask.shape[1:], jnp.int32),
            pltpu.SMEM((bound, rounds), jnp.int32),
            pltpu.VMEM(leaf_shape, BF16),
            pltpu.VMEM((leaves + received, points, channels), BF16),
            pltpu.VMEM((leaves + received, 8, 2 * points), F32),
            pltpu.VMEM((leaves, 8, 2 * points), F32),
            pltpu.VMEM((received, points, channels), BF16),
            pltpu.VMEM((received, 8, 2 * points), F32),
            pltpu.VMEM((3, leaves, points, 2 * points), F32),
            pltpu.VMEM(leaf_shape, BF16),
            pltpu.VMEM((leaves, kernels, points, near * points), BF16),
            pltpu.VMEM((leaves, kernels, points, channels), BF16),
            pltpu.VMEM((leaves, near * points, channels), F32),
            pltpu.VMEM((received, points, channels), BF16),
            pltpu.VMEM((received, points, channels), BF16),
            pltpu.VMEM((leaves, near * points, channels), BF16),
            pltpu.VMEM((kernels, leaves * points, channels), BF16),
            pltpu.VMEM((kernels, leaves * points, half), BF16),
            pltpu.VMEM((kernels, half, channels), BF16),
            pltpu.VMEM((kernels, half // narrow, channels), BF16),
            pltpu.VMEM((wide - 1, kernels, band, channels), BF16),
            pltpu.VMEM((kernels, band, channels), BF16),
            pltpu.VMEM((wide - 1, kernels, tile, channels), BF16),
            pltpu.VMEM((padded, tile, channels), BF16),
            pltpu.VMEM((CHUNKS, nz - 1, CHUNK // nz, tile, channels), BF16),
            pltpu.VMEM((CHUNKS, CHUNK // nz, tile, channels), BF16),
            pltpu.VMEM((padded, tile, channels), BF16),
            pltpu.VMEM((kernels, band, channels), BF16),
            pltpu.SemaphoreType.DMA((8,)),
            pltpu.SemaphoreType.DMA((copies,)),
            pltpu.SemaphoreType.DMA((copies,)),
        ],
        compiler_params=pltpu.CompilerParams(
            collective_id=0, has_side_effects=True, vmem_limit_bytes=48 * 1024 * 1024
        ),
        name="convolution",
    )(
        *(
            pltpu.with_memory_space_constraint(operand, pltpu.HBM)
            for operand in (
                features[0], coords.transpose(1, 0, 2), kernel_points.T, weights.reshape(cube), support_slot[0],
                slot_mask[0], send_leaf[0, 0].T, cotangent[0],
            )
        )
    )
    output, grad, grad_weight = pl.pallas_call(
        write_kernel,
        out_shape=(
            jax.ShapeDtypeStruct(leaf_shape, BF16),
            jax.ShapeDtypeStruct(leaf_shape, BF16),
            jax.ShapeDtypeStruct(cube, F32),
        ),
        in_specs=[vmem, vmem, vmem],
        out_specs=(hbm, hbm, hbm),
        scratch_shapes=[pltpu.VMEM(cube, F32), pltpu.SemaphoreType.DMA((2 + kernels,))],
        compiler_params=pltpu.CompilerParams(vmem_limit_bytes=16 * 1024 * 1024),
        name="write",
    )(output, grad, mean)
    return (output[None], grad[None], grad_weight.reshape(kernels * channels, channels))


def solution(mesh):
    in_specs = (
        P("rep", "dom", None, None),
        P("rep", None, "dom"),
        P(),
        P(),
        P("rep", "dom", None),
        P("rep", "dom", None, None, None),
        P("rep", "dom", None, None),
        P("rep", "dom", None, None),
    )
    out_specs = (P("rep", "dom", None, None), P("rep", "dom", None, None), P())
    return jax.shard_map(shards, mesh=mesh, in_specs=in_specs, out_specs=out_specs, check_vma=False)
```

```python
import functools

import jax
import jax.numpy as jnp
from jax import lax
from jax.experimental import pallas as pl
from jax.experimental.pallas import tpu as pltpu
from jax.sharding import PartitionSpec as P

QUANT = 0.0625
EPSILON = 1e-06
CORES = 2
NY = 4
CHUNK = 8
CHUNKS = 2
MESH = pl.DeviceIdType.MESH
F32, BF16 = jnp.float32, jnp.bfloat16


def place():
    dom, rep = lax.axis_index("dom"), lax.axis_index("rep")
    return rep // CORES, lax.rem(dom, NY), dom // NY, lax.rem(rep, CORES)


def device(x, y, z, core):
    return (z * NY + y, x * CORES + core)


def greet(others):
    barrier = pltpu.get_barrier_semaphore()
    for other in others:
        pl.semaphore_signal(barrier, inc=1, device_id=other, device_id_type=MESH)


def all_here(count):
    pl.semaphore_wait(pltpu.get_barrier_semaphore(), count)


def steps_of(count):
    return sorted(range(1, count), key=lambda step: -min(step, count - step))


def around(position, count):
    return [lax.rem(position + step, count) for step in steps_of(count)]


def product(left, right, dims):
    return lax.dot_general(left, right, (dims, ((), ())), preferred_element_type=F32)


def batches(nx):
    return 5 + 2 * CHUNKS * 8 + 2 * CHUNKS


def kernel(
    nx, nz, kernels, rounds,
    feats_in, coords_in, kernel_points_in, weights_in, slots_in, mask_in, sends_in, cot_in,
    output, grad, final,
    feats, coords, kernel_points, weights, slots, mask, sends, cot, pool_feats, pool_pos, own_pos, send_feats, send_pos, query, cot_pair, h, grad_summed, grad_support,
    send_grad, got_grad, support, summed, summed_pair, partial, partial_pair, got_first, part, got_second,
    slab, got_z, piece, gather_z, gather_second,
    local_sem, send_sem, recv_sem,
):
    leaves, points, channels = feats.shape
    near = slots.shape[1]
    bound = sends.shape[0]
    x, y, z, core = place()
    dom = z * NY + y
    sibling = device(x, y, z, 1 - core)
    axes = {
        "x": (x, nx, lambda o, c: device(o, y, z, c)),
        "y": (y, NY, lambda o, c: device(x, o, z, c)),
        "z": (z, nz, lambda o, c: device(x, y, o, c)),
    }
    low = NY.bit_length() - 1
    partners = []
    for bit in range(rounds):
        if bit < low:
            side = 1 << bit
            partners.append(device(x, y + side - 2 * side * lax.rem(y // side, 2), z, core))
        else:
            side = 1 << (bit - low)
            partners.append(device(x, y, z + side - 2 * side * lax.rem(z // side, 2), core))
    rings = {axis: [(to, o) for o in around(at, count)] for axis, (at, count, to) in axes.items()}
    plane = rings["x"] + rings["y"]

    @pl.when(core == 1)
    def _():
        greet([to(o, 1) for to, o in rings["z"] + plane] + [to(o, 0) for to, o in plane] + [sibling])

    @pl.when(core == 0)
    def _():
        greet(partners[::-1] + [to(o, 1) for to, o in plane] + [sibling])

    loads = {}
    for index, (name, src, dst) in enumerate((
        ("sends", sends_in, sends), ("coords", coords_in, coords), ("feats", feats_in, feats),
        ("cot", cot_in, cot), ("slots", slots_in, slots), ("points", kernel_points_in, kernel_points),
        ("weights", weights_in, weights), ("mask", mask_in, mask),
    )):
        loads[name] = pltpu.make_async_copy(src, dst, local_sem.at[index])
    early = ("sends", "coords", "feats")
    for name in early:
        loads[name].start()

    number = [0]

    def batch():
        number[0] += 1
        return number[0] - 1

    def describe(index, src, dst, other):
        return pltpu.make_async_remote_copy(
            src_ref=src, dst_ref=dst, send_sem=send_sem.at[index], recv_sem=recv_sem.at[index],
            device_id=other, device_id_type=MESH,
        )

    def push(index, src, dst, other):
        describe(index, src, dst, other).start()

    def arrived(index, like):
        pltpu.make_async_copy(like, like, recv_sem.at[index]).wait()

    def departed(index, like):
        pltpu.make_async_copy(like, like, send_sem.at[index]).wait()

    for name in early:
        loads[name].wait()
    for name in loads:
        if name not in early:
            loads[name].start()
    positions = coords[...].reshape(3, leaves * points).astype(F32) * QUANT
    for leaf in range(leaves):
        own = positions[:, leaf * points : (leaf + 1) * points]
        both = jnp.concatenate([own, own], 1)
        own_pos[leaf] = jnp.concatenate([both, jnp.zeros((8 - 3, 2 * points), F32)], 0)
        pool_pos[leaf] = own_pos[leaf]
        pool_feats[leaf] = feats[leaf]
    for bit in range(rounds):
        for t in range(bound):
            chosen = sends[t, bit]
            send_feats[bit * bound + t] = feats[chosen]
            send_pos[bit * bound + t] = own_pos[chosen]

    @pl.when(core == 1)
    def _():
        all_here(1 + 2 * len(plane) + len(rings["z"]))

    @pl.when(core == 0)
    def _():
        all_here(1 + len(partners) + len(plane))

    batch_pos, batch_feats, batch_cot, batch_far, batch_near = (batch() for _ in range(5))
    for bit in reversed(range(rounds)):
        entry, there = pl.ds(bit * bound, bound), pl.ds(leaves + bit * bound, bound)
        push(batch_pos, send_pos.at[entry], pool_pos.at[there], partners[bit])
    for bit in reversed(range(rounds)):
        entry, there = pl.ds(bit * bound, bound), pl.ds(leaves + bit * bound, bound)
        push(batch_feats, send_feats.at[entry], pool_feats.at[there], partners[bit])
    received = pl.ds(leaves, rounds * bound)
    loads["cot"].wait()
    copy_cot = describe(batch_cot, cot, cot_pair, sibling)
    copy_cot.start()

    rows = lax.broadcasted_iota(jnp.int32, (points, 2 * points), 0)
    lanes = lax.broadcasted_iota(jnp.int32, (points, 2 * points), 1)
    for leaf in range(leaves):
        for c in range(3):
            line = jnp.where(rows == lanes, pool_pos[leaf, c : c + 1, :], 0.0)
            query[c, leaf] = jnp.broadcast_to(jnp.sum(line, 1, keepdims=True), (points, 2 * points))

    loads["weights"].wait()

    upstream = cot[...].reshape(leaves * points, channels)
    for k in range(kernels):
        block = product(upstream, weights[k], ((1,), (1,)))
        grad_summed[:, k] = block.astype(BF16).reshape(leaves, points, channels)

    for name in ("slots", "points", "mask"):
        loads[name].wait()
    arrived(batch_pos, pool_pos.at[received])

    def correlate(leaf, _):
        for pair in range(near // 2):
            first = pool_pos[slots[leaf, 2 * pair]]
            second = pool_pos[slots[leaf, 2 * pair + 1]]
            lane = lax.broadcasted_iota(jnp.int32, first.shape, 1)
            places = jnp.where(lane < points, first, second)
            apart = [places[c : c + 1, :] - query[c, leaf] for c in range(3)]
            shown = jnp.concatenate([mask[leaf, 2 * pair], mask[leaf, 2 * pair + 1]], 1).astype(F32)

            for k in range(kernels):
                squared = jnp.full(shown.shape, EPSILON, F32)
                for c in range(3):
                    difference = apart[c] - kernel_points[c, k]
                    squared = squared + difference * difference
                weight = jnp.maximum(1.0 - squared * lax.rsqrt(squared), 0.0) * shown
                h[leaf, k, :, pair * 2 * points : (pair + 1) * 2 * points] = weight.astype(BF16)
        return 0

    lax.fori_loop(0, leaves, correlate, 0)

    half = channels // CORES
    own_half = pl.ds(pl.multiple_of(core * half, half), half)
    pair_half = pl.ds(pl.multiple_of((1 - core) * half, half), half)
    chunks = [(k0, min(CHUNK, kernels - k0)) for k0 in range(0, kernels, CHUNK)]
    groups = []
    for k0, nk in chunks:
        cut = (nk + 1) // 2
        if k0 == 0:
            groups.append([(k0, cut, "x", "y"), (k0 + cut, nk - cut, "y", "x")])
        else:
            groups.append([(k0, nk - cut, "y", "x"), (k0 + nk - cut, cut, "x", "y")])
    pairs = sum(groups, [])

    def band(axis, at, start=0):
        block = half // axes[axis][1]
        return pl.ds(pl.multiple_of(start + at * block, block), block)

    def tile(axis, at):
        block = part.shape[1] // axes[axis][1]
        return pl.ds(pl.multiple_of(at * block, block), block)

    halves, firsts, owns, fronts, back_own, lasts = ({} for _ in range(6))
    batch_first, batch_second, batch_back, batch_front = ({} for _ in range(4))
    for g0, ng, first, _ in pairs:
        there = pl.ds(g0, ng)
        at, count, to = axes[first]
        block = half // count
        halves[g0] = describe(batch(), summed.at[there, :, pair_half], summed_pair.at[there], sibling)
        for table in (batch_first, batch_second, batch_back, batch_front):
            table[g0] = batch()
        for step, o in zip(steps_of(count), around(at, count)):
            for side in range(CORES):
                rows = pl.ds(side * block, block)
                firsts[g0, step, side] = describe(
                    batch_first[g0], partial.at[there, band(first, o), :], got_first.at[step - 1, there, rows, :],
                    to(o, 1),
                )
                fronts[g0, step, side] = describe(
                    batch_front[g0], gather_second.at[there, rows, :],
                    final.at[there, band(first, at, side * half), :], to(o, side),
                )
        owns[g0] = describe(batch(), partial.at[there, band(first, at), :], partial_pair.at[there], sibling)
        back_own[g0] = describe(
            batch(), gather_second.at[there, pl.ds(0, block), :], final.at[there, band(first, at), :], sibling
        )
        here = final.at[there, own_half, :]
        lasts[g0] = describe(batch(), here, here, sibling)
    batch_z, batch_back_z = ([batch() for _ in chunks] for _ in range(2))

    def bands(g0, ng, first, count):
        return final.at[pl.ds(g0, ng), pl.ds(0, count * (half // axes[first][1])), :]

    arrived(batch_feats, pool_feats.at[received])
    for leaf in range(leaves):
        for n in range(near):
            support[leaf, n * points : (n + 1) * points, :] = pool_feats[slots[leaf, n]]
    for g0, ng, _, _ in pairs:
        for leaf in range(leaves):
            left = h[leaf, g0 : g0 + ng].reshape(ng * points, near * points)
            block = product(left, support[leaf], ((1,), (0,))).astype(BF16)
            summed[g0 : g0 + ng, leaf * points : (leaf + 1) * points, :] = block.reshape(ng, points, channels)
        halves[g0].start()

    copy_cot.wait_recv()
    upstream_pair = cot_pair[...].reshape(leaves * points, channels)
    for g0, ng, first, _ in pairs:
        halves[g0].wait_recv()
        for k in range(g0, g0 + ng):
            block = product(summed[k, :, own_half].T, upstream, ((1,), (0,)))
            block += product(summed_pair[k].T, upstream_pair, ((1,), (0,)))
            partial[k] = block.astype(BF16)
        for side in range(CORES):

            @pl.when(core == side)
            def _():
                for step in steps_of(axes[first][1]):
                    firsts[g0, step, side].start()
                if side == 0:
                    owns[g0].start()

    def gathered(entry, total):
        for leaf in range(leaves):
            for n in range(1, near):
                named = jnp.where(slots[leaf, n] == entry, 1.0, 0.0)
                total = total + named * grad_support[leaf, n * points : (n + 1) * points, :]
        return total

    def away(entry, _):
        send_grad[entry] = gathered(entry + leaves, jnp.zeros((points, channels), F32)).astype(BF16)
        return 0

    def feature_gradients():
        for leaf in range(leaves):
            left = h[leaf].reshape(kernels * points, near * points)
            right = grad_summed[leaf].reshape(kernels * points, channels)
            grad_support[leaf] = product(left, right, ((0,), (0,)))
        lax.fori_loop(0, rounds * bound, away, 0)

    def hand_back(index, bits):
        for bit in reversed(bits):
            entry = pl.ds(bit * bound, bound)
            push(index, send_grad.at[entry], got_grad.at[entry], partners[bit])

    far, near_by = pl.ds(low * bound, (rounds - low) * bound), pl.ds(0, low * bound)

    def handed_back():
        arrived(batch_far, got_grad.at[far])
        arrived(batch_near, got_grad.at[near_by])
        lax.fori_loop(0, leaves, owned, 0)
        departed(batch_far, send_grad.at[far])
        departed(batch_near, send_grad.at[near_by])
        departed(batch_pos, send_pos)
        departed(batch_feats, send_feats)
        copy_cot.wait_send()
        for copy in halves.values():
            copy.wait_send()

    def first_left():
        for g0, ng, first, _ in pairs:
            departed(batch_first[g0], bands(g0, ng, first, axes[first][1] - 1))

    def outputs():
        total = product(summed[0], weights[0], ((1,), (0,)))
        for k in range(1, kernels):
            total = total + product(summed[k], weights[k], ((1,), (0,)))
        output[...] = total.astype(BF16).reshape(output.shape)

    def owned(leaf, _):
        total = gathered(leaf, grad_support[leaf, 0:points, :])
        for bit in range(rounds):
            for t in range(bound):
                named = jnp.where(sends[t, bit] == leaf, 1.0, 0.0)
                total = total + named * got_grad[bit * bound + t].astype(F32)
        grad[leaf] = total.astype(BF16)
        return 0

    def exchange(side):
        for g0, ng, first, _ in pairs:
            count = axes[first][1]
            arrived(batch_front[g0], bands(g0, ng, first, count - 1))
            if side == 0:
                back_own[g0].wait_recv()
            lasts[g0].start()
        for g0, ng, first, _ in pairs:
            count = axes[first][1]
            if side == 1:
                back_own[g0].wait_send()
                departed(batch_front[g0], bands(g0, ng, first, CORES * (count - 1)))
            lasts[g0].wait_send()
        for copy in lasts.values():
            copy.wait_recv()

    feature_gradients()
    hand_back(batch_far, range(low, rounds))
    outputs()

    @pl.when(core == 0)
    def _():
        first_left()
        hand_back(batch_near, range(low))
        handed_back()
        for copy in owns.values():
            copy.wait_send()
        exchange(0)

    @pl.when(core == 1)
    def _():
        for g0, ng, first, second in pairs:
            at, count, _ = axes[first]
            block = half // count
            there = pl.ds(g0, ng)
            owns[g0].wait_recv()
            arrived(batch_first[g0], got_first.at[:, there])
            for k in range(g0, g0 + ng):
                for side, own in ((0, partial_pair[k]), (1, partial[k, band(first, at), :])):
                    rows = slice(side * block, (side + 1) * block)
                    total = own.astype(F32)
                    for step in range(count - 1):
                        total = total + got_first[step, k, rows, :].astype(F32)
                    part[k, rows, :] = total.astype(BF16)
            at, count, to = axes[second]
            for step, o in enumerate(around(at, count)):
                push(batch_second[g0], part.at[there, tile(second, o), :], got_second.at[step, there], to(o, 1))
        hand_back(batch_near, range(low))

        per_z = CHUNK // nz
        for index, (k0, nk) in enumerate(chunks):
            base = index * CHUNK - k0
            for k in range(k0 + nk, k0 + CHUNK):
                slab[base + k] = jnp.zeros(slab.shape[1:], BF16)
            for g0, ng, _, second in groups[index]:
                arrived(batch_second[g0], got_second.at[:, pl.ds(g0, ng)])
                at, count, _ = axes[second]
                for k in range(g0, g0 + ng):
                    total = part[k, tile(second, at), :].astype(F32)
                    for step in range(count - 1):
                        total = total + got_second[step, k].astype(F32)
                    slab[base + k] = total.astype(BF16)
            at, count, to = axes["z"]
            for step, o in enumerate(around(at, count)):
                push(batch_z[index], slab.at[pl.ds(index * CHUNK + o * per_z, per_z)], got_z.at[index, step], to(o, 1))
        devices = nx * NY * nz * CORES
        for index in range(CHUNKS):
            arrived(batch_z[index], got_z.at[index])
            at, count, to = axes["z"]
            own = pl.ds(index * CHUNK + z * per_z, per_z)
            total = slab[own].astype(F32)
            for step in range(count - 1):
                total = total + got_z[index, step].astype(F32)
            piece[index] = (total / devices).astype(BF16)
            for o in around(at, count):
                push(batch_back_z[index], piece.at[index], gather_z.at[own], to(o, 1))
            gather_z[own] = piece[index]

        handed_back()
        first_left()

        for index, (k0, nk) in enumerate(chunks):
            arrived(batch_back_z[index], got_z.at[index])
            for g0, ng, _, second in groups[index]:
                at, count, to = axes[second]
                there, here = pl.ds(g0, ng), pl.ds(index * CHUNK + g0 - k0, ng)
                own = tile(second, at)
                for o in around(at, count):
                    push(batch_back[g0], gather_z.at[here], gather_second.at[there, own, :], to(o, 1))
                gather_second[there, own, :] = gather_z[here]
        for g0, ng, first, _ in pairs:
            there = pl.ds(g0, ng)
            arrived(batch_back[g0], got_second.at[:, there])
            at, count, _ = axes[first]
            block = half // count
            for step in steps_of(count):
                for side in range(CORES):
                    fronts[g0, step, side].start()
            back_own[g0].start()
            final[there, band(first, at, half), :] = gather_second[there, block : CORES * block, :]
        for index in range(CHUNKS):
            departed(batch_z[index], got_z.at[index])
            departed(batch_back_z[index], got_z.at[index])
        for g0, ng, _, _ in pairs:
            departed(batch_second[g0], got_second.at[:, pl.ds(g0, ng)])
            departed(batch_back[g0], got_second.at[:, pl.ds(g0, ng)])
        exchange(1)


def write_kernel(output, grad, mean, output_out, grad_out, mean_out, wide, sem):
    copies = []
    for index, (src, dst) in enumerate(((output, output_out), (grad, grad_out))):
        copies.append(pltpu.make_async_copy(src, dst, sem.at[index]))
        copies[-1].start()
    for k in range(mean.shape[0]):
        wide[k] = mean[k].astype(F32)
        copies.append(pltpu.make_async_copy(wide.at[k], mean_out.at[k], sem.at[2 + k]))
        copies[-1].start()
    for copy in copies:
        copy.wait()


def shards(features, coords, kernel_points, weights, support_slot, slot_mask, send_leaf, cotangent):
    leaves, points, channels = features.shape[1:]
    kernels = kernel_points.shape[0]
    near = support_slot.shape[2]
    nx, nz = lax.axis_size("rep") // CORES, lax.axis_size("dom") // NY
    rounds = lax.axis_size("dom").bit_length() - 1
    bound = send_leaf.shape[3]
    received = rounds * bound
    padded = CHUNKS * CHUNK
    half = channels // CORES
    wide, narrow = max(nx, NY), min(nx, NY)
    band, tile = channels // narrow, channels // (nx * NY)
    copies = batches(max(nx, NY))
    vmem, hbm = (pl.BlockSpec(memory_space=space) for space in (pltpu.VMEM, pltpu.HBM))
    cube = (kernels, channels, channels)
    leaf_shape = (leaves, points, channels)
    output, grad, mean = pl.pallas_call(
        functools.partial(kernel, nx, nz, kernels, rounds),
        out_shape=(
            jax.ShapeDtypeStruct(leaf_shape, BF16),
            jax.ShapeDtypeStruct(leaf_shape, BF16),
            jax.ShapeDtypeStruct(cube, BF16),
        ),
        in_specs=[hbm] * 8,
        out_specs=(vmem, vmem, vmem),
        scratch_shapes=[
            pltpu.VMEM(leaf_shape, BF16),
            pltpu.VMEM((3, 1, leaves * points), jnp.int32),
            pltpu.SMEM((3, kernels), F32),
            pltpu.VMEM(cube, BF16),
            pltpu.SMEM((leaves, near), jnp.int32),
            pltpu.VMEM(slot_mask.shape[1:], jnp.int32),
            pltpu.SMEM((bound, rounds), jnp.int32),
            pltpu.VMEM(leaf_shape, BF16),
            pltpu.VMEM((leaves + received, points, channels), BF16),
            pltpu.VMEM((leaves + received, 8, 2 * points), F32),
            pltpu.VMEM((leaves, 8, 2 * points), F32),
            pltpu.VMEM((received, points, channels), BF16),
            pltpu.VMEM((received, 8, 2 * points), F32),
            pltpu.VMEM((3, leaves, points, 2 * points), F32),
            pltpu.VMEM(leaf_shape, BF16),
            pltpu.VMEM((leaves, kernels, points, near * points), BF16),
            pltpu.VMEM((leaves, kernels, points, channels), BF16),
            pltpu.VMEM((leaves, near * points, channels), F32),
            pltpu.VMEM((received, points, channels), BF16),
            pltpu.VMEM((received, points, channels), BF16),
            pltpu.VMEM((leaves, near * points, channels), BF16),
            pltpu.VMEM((kernels, leaves * points, channels), BF16),
            pltpu.VMEM((kernels, leaves * points, half), BF16),
            pltpu.VMEM((kernels, half, channels), BF16),
            pltpu.VMEM((kernels, half // narrow, channels), BF16),
            pltpu.VMEM((wide - 1, kernels, band, channels), BF16),
            pltpu.VMEM((kernels, band, channels), BF16),
            pltpu.VMEM((wide - 1, kernels, tile, channels), BF16),
            pltpu.VMEM((padded, tile, channels), BF16),
            pltpu.VMEM((CHUNKS, nz - 1, CHUNK // nz, tile, channels), BF16),
            pltpu.VMEM((CHUNKS, CHUNK // nz, tile, channels), BF16),
            pltpu.VMEM((padded, tile, channels), BF16),
            pltpu.VMEM((kernels, band, channels), BF16),
            pltpu.SemaphoreType.DMA((8,)),
            pltpu.SemaphoreType.DMA((copies,)),
            pltpu.SemaphoreType.DMA((copies,)),
        ],
        compiler_params=pltpu.CompilerParams(
            collective_id=0, has_side_effects=True, vmem_limit_bytes=48 * 1024 * 1024
        ),
        name="convolution",
    )(
        *(
            pltpu.with_memory_space_constraint(operand, pltpu.HBM)
            for operand in (
                features[0], coords.transpose(1, 0, 2), kernel_points.T, weights.reshape(cube), support_slot[0],
                slot_mask[0], send_leaf[0, 0].T, cotangent[0],
            )
        )
    )
    output, grad, grad_weight = pl.pallas_call(
        write_kernel,
        out_shape=(
            jax.ShapeDtypeStruct(leaf_shape, BF16),
            jax.ShapeDtypeStruct(leaf_shape, BF16),
            jax.ShapeDtypeStruct(cube, F32),
        ),
        in_specs=[vmem, vmem, vmem],
        out_specs=(hbm, hbm, hbm),
        scratch_shapes=[pltpu.VMEM(cube, F32), pltpu.SemaphoreType.DMA((2 + kernels,))],
        compiler_params=pltpu.CompilerParams(vmem_limit_bytes=16 * 1024 * 1024),
        name="write",
    )(output, grad, mean)
    return (output[None], grad[None], grad_weight.reshape(kernels * channels, channels))


def solution(mesh):
    in_specs = (
        P("rep", "dom", None, None),
        P("rep", None, "dom"),
        P(),
        P(),
        P("rep", "dom", None),
        P("rep", "dom", None, None, None),
        P("rep", "dom", None, None),
        P("rep", "dom", None, None),
    )
    out_specs = (P("rep", "dom", None, None), P("rep", "dom", None, None), P())
    return jax.shard_map(shards, mesh=mesh, in_specs=in_specs, out_specs=out_specs, check_vma=False)
```
